256 devices in a mesh: dp: 16 (over z_lo, y, core), feat: 16 (over x, z_hi).
Axes of the slice: x: 4, y: 4, z: 8 (z_hi: 4, z_lo: 2; z = z_hi * 2 + z_lo), core: 2. Of those that a mesh axis runs over, the one named last changes fastest.
Arguments:
- images: bfloat16 [6144, 3072], P('dp'), may hold values from -6 to 6
- labels: int32 [6144], P('dp'), may hold values from 0 to 9
- frequencies: bfloat16 [3072, 16384], P(None, 'feat'), may hold values from -0.15625 to 0.15625
- privacy_noise: float32 [10, 2, 16384], P(None, None, 'feat'), may hold values from -0.6 to 0.6
- latents: bfloat16 [4096, 256], P('dp'), may hold values from -6 to 6
- gen_labels: int32 [4096], P('dp'), may hold values from 0 to 9
- gen_in: bfloat16 [256, 1024], replicated, may hold values from -0.375 to 0.375
- gen_out: bfloat16 [1024, 3072], replicated, may hold values from -0.25 to 0.25
Outputs:
- match_loss: float32 [], replicated
- grad_in: float32 [256, 1024], P('dp')
- grad_out: float32 [1024, 3072], P('dp')
The draws below stay inside these ranges and needn't reach their ends.
All inputs are finite; a program needn't handle non-finite values.
Results may differ from the reference program's by a relative error of at most 0.0035.
Values sent between devices are 32-bit elements; how exact they have to be, the bound alone decides.
A program may use at most 128 MiB of HBM per device.

```python
import jax
import jax.numpy as jnp
from jax import lax

D = 3072
CLASSES = 10
HID = 1024
ZDIM = 256
IMAGES = 6144
GEN = 4096
FEATS = 16384


def set_ends(values, own_key, smallest, largest):
    spot = [jax.random.randint(jax.random.fold_in(own_key, axis), (), 0, length) for axis, length in enumerate(values.shape)]
    widest = values.shape.index(max(values.shape))
    neighbour = spot[:widest] + [(spot[widest] + 1) % values.shape[widest]] + spot[widest + 1:]
    return values.at[tuple(spot)].set(smallest).at[tuple(neighbour)].set(largest)


def shard_levels(stream_key, shape, shards, smallest, high):
    def one(dim, parts):
        steps = jax.random.uniform(jax.random.fold_in(jax.random.fold_in(stream_key, 6), dim), (parts,), jnp.float32, smallest / len(shards), high / len(shards))
        return jnp.repeat(jnp.exp(steps), shape[dim] // parts).reshape((-1,) + (1,) * (len(shape) - dim - 1))

    factor_of = one(*shards[0])
    for cut in shards[1:]:
        factor_of = factor_of * one(*cut)
    return factor_of


def gaussian(key, extent, scale, most, pieces=(), held_as=jnp.bfloat16):
    gain = shard_levels(key, extent, pieces, -0.22, 0.18) if pieces else 1.0
    array = jax.random.normal(key, extent, jnp.float32) * scale * gain
    return jnp.minimum(jnp.maximum(array, -most), most).astype(held_as)


def setup_inputs(seed: int = 0) -> dict:
    splits = jax.random.split(jax.random.key(seed), 9)
    return {
        "images": gaussian(splits[0], (IMAGES, D), 1.0, 6.0, ((0, 16),)),
        "labels": set_ends(jax.random.randint(splits[1], (IMAGES,), 0, CLASSES), jax.random.fold_in(splits[1], 1), 0, CLASSES - 1).astype(jnp.int32),
        "frequencies": gaussian(splits[2], (D, FEATS), (D // 2) ** -0.5, 0.15625, ((1, 16),)),
        "privacy_noise": gaussian(splits[3], (CLASSES, 2, FEATS), 0.1, 0.6, ((2, 16),), jnp.float32),
        "latents": gaussian(splits[4], (GEN, ZDIM), 1.0, 6.0, ((0, 16),)),
        "gen_labels": set_ends(jax.random.randint(splits[5], (GEN,), 0, CLASSES), jax.random.fold_in(splits[5], 1), 0, CLASSES - 1).astype(jnp.int32),
        "gen_in": gaussian(splits[6], (ZDIM, HID), ZDIM ** -0.5, 0.375),
        "gen_out": gaussian(splits[7], (HID, D), (HID // 2) ** -0.5, 0.25),
    }


def class_means(phase, classes_of, count):
    feats = jnp.concatenate([jnp.cos(phase), jnp.sin(phase)], axis=1)
    onehot = (classes_of[:, None] == jnp.arange(CLASSES)[None, :]).astype(jnp.float32)
    sums = jnp.dot(onehot.T, feats, precision=lax.Precision.HIGHEST) * (CLASSES / count)
    return sums.reshape(CLASSES, 2, FEATS), onehot


def reference(images, labels, frequencies, privacy_noise, latents, gen_labels, gen_in, gen_out):
    data_phase = jnp.dot(images, frequencies, preferred_element_type=jnp.float32)
    data_mean, unused = class_means(data_phase, labels, IMAGES)
    pre_hidden = jnp.dot(latents, gen_in, preferred_element_type=jnp.float32)
    sigmoid_h = jax.nn.sigmoid(pre_hidden)
    hidden = (pre_hidden * sigmoid_h).astype(jnp.bfloat16)
    image_out = jnp.tanh(jnp.dot(hidden, gen_out, preferred_element_type=jnp.float32))
    gen_image = image_out.astype(jnp.bfloat16)
    gen_phase = jnp.dot(gen_image, frequencies, preferred_element_type=jnp.float32)
    gen_mean, gen_onehot = class_means(gen_phase, gen_labels, GEN)
    mean_gap = gen_mean - (data_mean + privacy_noise)
    match_loss = jnp.sum(mean_gap * mean_gap) / (2.0 * FEATS)
    gap_rows = jnp.dot(gen_onehot, mean_gap.reshape(CLASSES, 2 * FEATS), precision=lax.Precision.HIGHEST) * (16.0 * CLASSES / GEN)
    phase_grad = (jnp.cos(gen_phase) * gap_rows[:, FEATS:] - jnp.sin(gen_phase) * gap_rows[:, :FEATS]).astype(jnp.bfloat16)
    image_grad = jnp.dot(phase_grad, frequencies.T, preferred_element_type=jnp.float32)
    out_grad = (image_grad * (1.0 - image_out * image_out)).astype(jnp.bfloat16)
    grad_out = jnp.dot(hidden.T, out_grad, preferred_element_type=jnp.float32)
    back_hidden = jnp.dot(out_grad, gen_out.T, preferred_element_type=jnp.float32)
    hidden_grad = (back_hidden * sigmoid_h * (1.0 + pre_hidden * (1.0 - sigmoid_h))).astype(jnp.bfloat16)
    grad_in = jnp.dot(latents.T, hidden_grad, preferred_element_type=jnp.float32)
    return match_loss, grad_in, grad_out
```

```python
import functools

import jax
import jax.numpy as jnp
from jax import lax
from jax.experimental import pallas as pl
from jax.experimental.pallas import tpu as pltpu
from jax.sharding import PartitionSpec as P

MESH = pl.DeviceIdType.MESH
F32 = jnp.float32
BF16 = jnp.bfloat16

SIN = (6.28318284102346, -41.34142273936724, 81.59620932441723, -76.58030929887768, 41.20616782312917, -12.272323133322006)
COS = (0.999999989172567, -19.73920453212146, 64.93911898457917, -85.45016555726593, 60.16783176141255, -25.968313346422505, 6.5296104065360066)

N, D, FL, HID, Z, NI = 256, 3072, 1024, 1024, 256, 384
ROWS = N + NI
SUBS = (96, 96)
STARTS = (0, 96)
NS = len(SUBS)
Q = 4 * NS
LAG = 2
NT = (((1,), (1,)), ((), ()))


def poly(coeffs, u):
    r = coeffs[-1] * u + coeffs[-2]
    for c in coeffs[-3::-1]:
        r = r * u + c
    return r


def cos_sin(phase):
    t = phase * 0.15915494309189535
    f = t - jnp.round(t)
    u = f * f
    return poly(COS, u), f * poly(SIN, u)


def split(v):
    hi = v.astype(BF16)
    return hi, (v - hi.astype(F32)).astype(BF16)


def mm(a, b):
    return jnp.dot(a, b, preferred_element_type=F32)


def mmt(a, b):
    return lax.dot_general(a, b, NT, preferred_element_type=F32)


def kernel(images_h, freq_h, gen_out_h, lab_ref, glab_ref, noise_ref, lat_ref, gin_ref,
           loss_ref, gi_ref, go_ref,
           freq, gout, lhs, noise, hidden, q_s, qt, s_s, st, latt, oneh, onet, cosg, sing, gp, rsb, gapb, pg,
           part, ohi, olo, hgt, gin, xa, xb, za, zb, gic, gid, gix, giz, gig, lvx, lvz, gt_p, goc, god, gfull,
           lsem, ar_s, ar_r, xa_s, xa_r, xb_s, xb_r, za_s, za_r, zb_s, zb_r, g1_s, g1_r, gd_s, gd_r,
           gx_s, gx_r, gz_s, gz_r, gzg_s, gzg_r, gxg_s, gxg_r, lx_s, lx_r, lz_s, lz_r,
           oc_s, oc_r, od_s, od_r, oz_s, oz_r, ox_s, ox_r, oe_s, oe_r):
    dp = lax.axis_index("dp")
    ft = lax.axis_index("feat")
    core = lax.rem(dp, 2)
    chip = dp // 2
    x = ft // 4
    zh = lax.rem(ft, 4)

    def xdev(k):
        return (dp, lax.rem(x + k, 4) * 4 + zh)

    def zdev(k):
        return (dp, x * 4 + lax.rem(zh + k, 4))

    def cdev(k):
        return (lax.rem(chip + k, 8) * 2 + core, ft)

    other = (chip * 2 + 1 - core, ft)

    def remote(src, dst, ss, rs, dev):
        return pltpu.make_async_remote_copy(src_ref=src, dst_ref=dst, send_sem=ss, recv_sem=rs, device_id=dev, device_id_type=MESH)

    loads = [pltpu.make_async_copy(gen_out_h, gout, lsem.at[0]), pltpu.make_async_copy(images_h, lhs.at[pl.ds(N, NI)], lsem.at[1])]
    for n in range(4):
        loads.append(pltpu.make_async_copy(freq_h.at[:, pl.ds(n * 256, 256)], freq.at[:, pl.ds(n * 256, 256)], lsem.at[2 + n]))
    for c in loads:
        c.start()

    bar = pltpu.get_barrier_semaphore()

    def greet_dp(k, carry):
        pl.semaphore_signal(bar, inc=1, device_id=(lax.rem(dp + k, 16), ft), device_id_type=MESH)
        return carry

    lax.fori_loop(1, 16, greet_dp, 0)
    for k in (1, 2, 3):
        pl.semaphore_signal(bar, inc=1, device_id=xdev(k), device_id_type=MESH)
        pl.semaphore_signal(bar, inc=1, device_id=zdev(k), device_id_type=MESH)

    noise[...] = jnp.zeros_like(noise)
    for k in range(2):
        noise[16 * k : 16 * k + 10, :] = noise_ref[:, k, :]
    cls = lax.broadcasted_iota(jnp.int32, (32, N), 0)
    on_g = (jnp.where(cls < 16, cls, cls - 16) == glab_ref[...]).astype(F32)
    cls_g = lax.broadcasted_iota(jnp.int32, (16, N), 0)
    oneh[0:16, 0:N] = (cls_g == glab_ref[...]).astype(F32).astype(BF16)
    oneh[16:32, 0:N] = jnp.zeros((16, N), BF16)
    cls_d = lax.broadcasted_iota(jnp.int32, (16, NI), 0)
    oneh[0:16, N:ROWS] = jnp.zeros((16, NI), BF16)
    oneh[16:32, N:ROWS] = (cls_d == lab_ref[...]).astype(F32).astype(BF16)
    onet[...] = jnp.concatenate([on_g, jnp.zeros((96, N), F32)], axis=0).T.astype(BF16)
    latt[...] = lat_ref[...].astype(F32).T.astype(BF16)

    pre = mm(lat_ref[...], gin_ref[...])
    sig = jax.nn.sigmoid(pre)
    hidden[...] = (pre * sig).astype(BF16)
    s_s[...] = sig * (1.0 + pre * (1.0 - sig))
    loads[0].wait()

    def gen(n, carry):
        cols = pl.ds(pl.multiple_of(n * 512, 512), 512)
        out = jnp.tanh(mm(hidden[...], gout[:, cols]))
        lhs[0:N, cols] = out.astype(BF16)
        q_s[:, cols] = 1.0 - out * out
        return carry

    lax.fori_loop(0, 6, gen, 0)
    loads[1].wait()

    def phases(n):
        loads[2 + n].wait()
        cols = slice(n * 256, n * 256 + 256)
        ph = mm(lhs[...], freq[:, cols])
        cs, sn = cos_sin(ph)
        cosg[:, cols] = cs[0:N]
        sing[:, cols] = sn[0:N]
        for k, v in ((0, cs), (1, sn)):
            hi, lo = split(v)
            sums = mm(oneh[...], hi) + mm(oneh[...], lo)
            gp[16 * k : 16 * k + 16, cols] = sums[0:16] * (10.0 / 4096.0) - sums[16:32] * (10.0 / 6144.0)

    def block(o):
        return pl.multiple_of(8 * (o // 4), 8), pl.multiple_of(128 * lax.rem(o, 4), 128)

    row_me, lane_me = block(dp)

    def rs_copy(h, peer):
        r, l = block(peer)
        src = gp.at[pl.ds(r, 8), pl.ds(pl.multiple_of(h * 512 + l, 128), 128)]
        return src

    def ar_send(h):
        rsb[h, dp] = gp[pl.ds(row_me, 8), pl.ds(pl.multiple_of(h * 512 + lane_me, 128), 128)]

        def go(k, carry):
            peer = lax.rem(dp + k, 16)
            remote(rs_copy(h, peer), rsb.at[h, dp], ar_s.at[h, 0, peer], ar_r.at[h, 0, dp], (peer, ft)).start()
            return carry

        lax.fori_loop(1, 16, go, 0)

    def ar_wait(h, which):
        def go(k, carry):
            peer = lax.rem(dp + k, 16)
            if which == 0:
                d = remote(rs_copy(h, peer), rsb.at[h, peer], ar_s.at[h, 0, peer], ar_r.at[h, 0, peer], (peer, ft))
            else:
                r, l = block(peer)
                d = remote(gapb.at[h, pl.ds(row_me, 8), pl.ds(lane_me, 128)], gapb.at[h, pl.ds(r, 8), pl.ds(l, 128)],
                           ar_s.at[h, 1, peer], ar_r.at[h, 1, peer], (peer, ft))
            d.wait_recv()
            d.wait_send()
            return carry

        lax.fori_loop(1, 16, go, 0)

    def ar_spread(h):
        ar_wait(h, 0)
        mine = gapb.at[h, pl.ds(row_me, 8), pl.ds(lane_me, 128)]
        mine[...] = jnp.sum(rsb[h], axis=0)

        def go(k, carry):
            peer = lax.rem(dp + k, 16)
            remote(mine, mine, ar_s.at[h, 1, peer], ar_r.at[h, 1, dp], (peer, ft)).start()
            return carry

        lax.fori_loop(1, 16, go, 0)

    def gap(h):
        ar_wait(h, 1)
        cols = slice(h * 512, h * 512 + 512)
        g = gapb[h] - noise[:, cols]
        sq = g * g
        lv = sq[0:8] + sq[8:16] + sq[16:24] + sq[24:32]
        lv = lv[:, 0:128] + lv[:, 128:256] + lv[:, 256:384] + lv[:, 384:512]
        hi, lo = split(g * (160.0 / 4096.0))
        g0 = mm(onet[:, 0:32], jnp.concatenate([hi[0:16], lo[0:16]], axis=0))
        g1 = mm(onet[:, 0:32], jnp.concatenate([hi[16:32], lo[16:32]], axis=0))
        pg[:, cols] = (cosg[:, cols] * g1 - sing[:, cols] * g0).astype(BF16)
        return lv

    phases(0)
    phases(1)
    pl.semaphore_wait(bar, 21)
    ar_send(0)
    phases(2)
    ar_spread(0)
    phases(3)
    ar_send(1)

    def turn_q(n, carry):
        o = pl.multiple_of(n * 256, 256)
        qt[pl.ds(o, 256), :] = q_s[:, pl.ds(o, 256)].T
        return carry

    lax.fori_loop(0, 12, turn_q, 0)
    lv = gap(0)

    def first_half(n, carry):
        rows = pl.ds(pl.multiple_of(n * 768, 256), 768)
        part[rows, :] = mmt(freq[rows, 0:512], pg[:, 0:512])
        return carry

    lax.fori_loop(0, 4, first_half, 0)
    ar_spread(1)

    def turn_s(n, carry):
        o = pl.multiple_of(n * 256, 256)
        st[pl.ds(o, 256), :] = s_s[:, pl.ds(o, 256)].T
        return carry

    lax.fori_loop(0, 4, turn_s, 0)
    lv = lv + gap(1)

    def part_rows(xr, k, s, half, rows):
        zq = lax.rem(zh + (2, 1, 3, 0)[k], 4)
        base = lax.rem(x + xr, 4) * 768 + zq * 192 + STARTS[s] + half
        return part.at[pl.ds(pl.multiple_of(base, 8), rows), :]

    def second_half(xr):
        rows = pl.ds(pl.multiple_of(lax.rem(x + xr, 4) * 768, 256), 768)
        part[rows, :] += mmt(freq[rows, 512:1024], pg[:, 512:1024])

    def qk(q):
        return q // 4, q % 4

    def xa_copy(q, b):
        s, k = qk(q)
        w = SUBS[s] // 2
        return remote(part_rows(2, k, s, b * w, w), xa.at[q, b, pl.ds(0, w)], xa_s.at[q, b], xa_r.at[q, b], xdev((1, 3)[b]))

    def xb_copy(q, b):
        s, k = qk(q)
        w = SUBS[s]
        return remote(part_rows((1, 3)[b], k, s, 0, w), xb.at[q, b, pl.ds(0, w)], xb_s.at[q, b], xb_r.at[q, b], xdev((1, 3)[b]))

    def za_copy(s, b):
        w = SUBS[s] // 2
        return remote(part_rows(0, 0, s, b * w, w), za.at[s, b, pl.ds(0, w)], za_s.at[s, b], za_r.at[s, b], zdev((1, 3)[b]))

    def zb_copy(s, b):
        w = SUBS[s]
        return remote(part_rows(0, 1 + b, s, 0, w), zb.at[s, b, pl.ds(0, w)], zb_s.at[s, b], zb_r.at[s, b], zdev((1, 3)[b]))

    sent = []
    second_half(2)
    for q in range(Q):
        for b in range(2):
            c = xa_copy(q, b)
            c.start()
            sent.append(c)

    lvx[x] = lv
    for k in (1, 2, 3):
        peer = lax.rem(x + k, 4)
        c = remote(lvx.at[x], lvx.at[x], lx_s.at[peer], lx_r.at[x], xdev(k))
        c.start()
        sent.append(c)

    for xr in (1, 3, 0):
        second_half(xr)

    def factor(n, carry):
        rows = pl.ds(pl.multiple_of(n * 256, 256), 256)
        hi, lo = split(part[rows, :] * qt[rows, :])
        ohi[rows, :] = hi
        olo[rows, :] = lo
        return carry

    lax.fori_loop(0, 12, factor, 0)

    def s2(q):
        s, k = qk(q)
        w = SUBS[s] // 2
        for b in range(2):
            xa_copy(q, b).wait_recv()
            r = part_rows((1, 3)[b], k, s, b * w, w)
            r[...] = r[...] + xa[q, b, 0:w]
            c = xb_copy(q, b)
            c.start()
            sent.append(c)

    def s3(q):
        s, k = qk(q)
        w = SUBS[s]
        h = w // 2
        for b in range(2):
            xb_copy(q, b).wait_recv()
        r = part_rows(0, k, s, 0, w)
        r[...] = r[...] + xb[q, 0, 0:w] + xb[q, 1, 0:w]
        if k == 0:
            for b in range(2):
                c = za_copy(s, b)
                c.start()
                sent.append(c)
        elif k < 3:
            b = k - 1
            za_copy(s, b).wait_recv()
            r = part_rows(0, k, s, b * h, h)
            r[...] = r[...] + za[s, b, 0:h]
            c = zb_copy(s, b)
            c.start()
            sent.append(c)
        else:
            for b in range(2):
                zb_copy(s, b).wait_recv()
            own = r[...] + zb[s, 0, 0:w] + zb[s, 1, 0:w]
            base = pl.multiple_of(ft * 192 + STARTS[s], 8)
            og = (own * qt[pl.ds(base, w), :]).astype(BF16)
            gt_p[s, 0:w, :] = mm(og, hidden[...])
            c = oc_copy(s)
            c.start()
            sent.append(c)

    def oc_copy(s):
        h = SUBS[s] // 2
        return remote(gt_p.at[s, pl.ds(pl.multiple_of((1 - core) * h, 8), h)], goc.at[s, pl.ds(0, h)], oc_s.at[s], oc_r.at[s], other)

    def od_copy(s, k, mine):
        h = SUBS[s] // 2
        peer = lax.rem(chip + k, 8)
        return remote(gt_p.at[s, pl.ds(pl.multiple_of(core * h, 8), h), pl.ds(pl.multiple_of(peer * 128, 128), 128)],
                      god.at[s, chip if mine else peer, pl.ds(0, h)], od_s.at[s, peer], od_r.at[s, chip if mine else peer], cdev(k))

    def rows_of(s, c):
        h = SUBS[s] // 2
        return pl.ds(pl.multiple_of(STARTS[s] + c * h, 8), h)

    def oz_copy(s, k, mine):
        peer = lax.rem(zh + k, 4)
        src = zh if mine else peer
        at = gfull.at[x * 4 + src, rows_of(s, core), :]
        return remote(at, at, oz_s.at[s, peer], oz_r.at[s, src], zdev(k))

    def ox_copy(s, k, mine):
        peer = lax.rem(x + k, 4)
        src = x if mine else peer
        at = gfull.at[pl.ds(src * 4, 4), rows_of(s, core), :]
        return remote(at, at, ox_s.at[s, peer], ox_r.at[s, src], xdev(k))

    def oe_copy(s, c):
        at = gfull.at[:, rows_of(s, c), :]
        return remote(at, at, oe_s.at[s], oe_r.at[s], other)

    def start_all(copies):
        for c in copies:
            c.start()
            sent.append(c)

    def go1(s):
        h = SUBS[s] // 2
        oc_copy(s).wait_recv()
        r = gt_p.at[s, pl.ds(pl.multiple_of(core * h, 8), h)]
        r[...] = r[...] + goc[s, 0:h]
        start_all([od_copy(s, k, True) for k in range(1, 8)])
        god[s, chip, 0:h] = gt_p[s, pl.ds(pl.multiple_of(core * h, 8), h), pl.ds(pl.multiple_of(chip * 128, 128), 128)]

    def go2(s):
        h = SUBS[s] // 2
        for k in range(1, 8):
            od_copy(s, k, False).wait_recv()
        gfull[ft, rows_of(s, core), :] = jnp.sum(god[s, :, 0:h], axis=0)
        start_all([oz_copy(s, k, True) for k in (1, 3, 2)])

    def go3(s):
        for k in (1, 3, 2):
            oz_copy(s, k, False).wait_recv()
        start_all([ox_copy(s, k, True) for k in (1, 3, 2)])

    def go4(s):
        for k in (1, 3, 2):
            ox_copy(s, k, False).wait_recv()
        start_all([oe_copy(s, core)])

    def back(n, carry):
        rows = pl.ds(pl.multiple_of(n * 256, 256), 256)
        bh = mm(gout[rows, :], ohi[...]) + mm(gout[rows, :], olo[...])
        hi, lo = split(bh * st[rows, :])
        g = mmt(latt[...], hi) + mmt(latt[...], lo)
        gin[:, :, :, rows] = g.reshape(8, 2, 16, 256)
        return carry

    def gi0():
        lax.fori_loop(0, 4, back, 0)
        start_all([g1_copy()])

    def g1_copy():
        return remote(gin.at[:, 1 - core], gic, g1_s.at[0], g1_r.at[0], other)

    def gd_copy(k, mine):
        peer = lax.rem(chip + k, 8)
        src = chip if mine else peer
        return remote(gin.at[peer, core], gid.at[src], gd_s.at[peer], gd_r.at[src], cdev(k))

    def gi1():
        g1_copy().wait_recv()
        gin[:, core] = gin[:, core] + gic[...]
        start_all([gd_copy(k, True) for k in range(1, 8)])
        gid[chip] = gin[chip, core]

    def gx_copy(k, mine):
        peer = lax.rem(x + k, 4)
        src = x if mine else peer
        return remote(gid.at[chip, :, pl.ds(pl.multiple_of(peer * 256, 256), 256)], gix.at[src], gx_s.at[peer], gx_r.at[src], xdev(k))

    def gi2():
        for k in range(1, 8):
            gd_copy(k, False).wait_recv()
        total = jnp.sum(gid[...], axis=0)
        gid[chip] = total
        start_all([gx_copy(k, True) for k in (1, 3, 2)])
        gix[x] = gid[chip, :, pl.ds(pl.multiple_of(x * 256, 256), 256)]
        for k in (1, 2, 3):
            peer = lax.rem(x + k, 4)
            remote(lvx.at[x], lvx.at[peer], lx_s.at[peer], lx_r.at[peer], xdev(k)).wait_recv()
        lvz[zh] = jnp.sum(lvx[...], axis=0)
        for k in (1, 2, 3):
            peer = lax.rem(zh + k, 4)
            start_all([remote(lvz.at[zh], lvz.at[zh], lz_s.at[peer], lz_r.at[zh], zdev(k))])

    def zblock(p):
        return pl.ds(pl.multiple_of(8 * (p // 2), 8), 8), pl.ds(pl.multiple_of(128 * lax.rem(p, 2), 128), 128)

    def gz_copy(k, mine):
        peer = lax.rem(zh + k, 4)
        src = zh if mine else peer
        r, l = zblock(peer)
        return remote(gix.at[x, r, l], giz.at[src], gz_s.at[peer], gz_r.at[src], zdev(k))

    def gi3():
        for k in (1, 3, 2):
            gx_copy(k, False).wait_recv()
        total = jnp.sum(gix[...], axis=0)
        gix[x] = total
        start_all([gz_copy(k, True) for k in (1, 3, 2)])
        r, l = zblock(zh)
        giz[zh] = gix[x, r, l]

    def gzg_copy(k, mine):
        peer = lax.rem(zh + k, 4)
        src = zh if mine else peer
        r, l = zblock(src)
        return remote(gig.at[x, r, l], gig.at[x, r, l], gzg_s.at[peer], gzg_r.at[src], zdev(k))

    def gi4():
        for k in (1, 3, 2):
            gz_copy(k, False).wait_recv()
        r, l = zblock(zh)
        gig[x, r, l] = jnp.sum(giz[...], axis=0)
        start_all([gzg_copy(k, True) for k in (1, 3, 2)])

    def gxg_copy(k, mine):
        peer = lax.rem(x + k, 4)
        src = x if mine else peer
        return remote(gig.at[src], gig.at[src], gxg_s.at[peer], gxg_r.at[src], xdev(k))

    def gi5():
        for k in (1, 3, 2):
            gzg_copy(k, False).wait_recv()
        start_all([gxg_copy(k, True) for k in (1, 3, 2)])

    def gi6():
        for k in (1, 3, 2):
            gxg_copy(k, False).wait_recv()
        for p in range(4):
            gi_ref[:, p * 256 : p * 256 + 256] = gig[p]
        for k in (1, 2, 3):
            peer = lax.rem(zh + k, 4)
            remote(lvz.at[zh], lvz.at[peer], lz_s.at[peer], lz_r.at[peer], zdev(k)).wait_recv()
        loss_ref[...] = jnp.sum(jnp.sum(lvz[...], axis=0), axis=(0, 1), keepdims=True) * (1.0 / 32768.0)

    gi0()
    s2(0)
    s2(1)
    gi1()
    s2(2)
    s3(0)
    s2(3)
    s3(1)
    s2(4)
    s3(2)
    s2(5)
    s3(3)
    s2(6)
    s3(4)
    gi2()
    go1(0)
    s2(7)
    s3(5)
    gi3()
    go2(0)
    s3(6)
    s3(7)
    go1(1)
    gi4()
    go3(0)
    gi5()
    go2(1)
    go4(0)
    gi6()
    go3(1)
    go4(1)
    for s in range(NS):
        oe_copy(s, 1 - core).wait_recv()

    def turn(p, carry):
        v = gfull[pl.ds(p * 2, 2)].reshape(384, 128).T
        go_ref[:, pl.ds(pl.multiple_of(p * 384, 128), 384)] = jnp.where(core == 0, v[0:64], v[64:128])
        return carry

    lax.fori_loop(0, 8, turn, 0)
    for c in sent:
        c.wait_send()


def per_device(images, labels, frequencies, privacy_noise, latents, gen_labels, gen_in, gen_out):
    vm = pl.BlockSpec(memory_space=pltpu.VMEM)
    hb = pl.BlockSpec(memory_space=pltpu.HBM)
    V = pltpu.VMEM
    dma = pltpu.SemaphoreType.DMA
    w = max(SUBS)
    h = w // 2
    scratch = [
        V((D, FL), BF16), V((HID, D), BF16), V((ROWS, D), BF16), V((32, FL), F32), V((N, HID), BF16),
        V((N, D), F32), V((D, N), F32), V((N, HID), F32), V((HID, N), F32), V((Z, N), BF16),
        V((32, ROWS), BF16), V((N, 128), BF16), V((N, FL), F32), V((N, FL), F32), V((32, FL), F32),
        V((2, 16, 8, 128), F32), V((2, 32, 512), F32), V((N, FL), BF16),
        V((D, N), F32), V((D, N), BF16), V((D, N), BF16), V((8, 128), F32), V((8, 2, 16, HID), F32),
        V((Q, 2, h, N), F32), V((Q, 2, w, N), F32), V((NS, 2, h, N), F32), V((NS, 2, w, N), F32),
        V((8, 16, HID), F32), V((8, 16, HID), F32), V((4, 16, 256), F32), V((4, 8, 128), F32), V((4, 16, 256), F32),
        V((4, 8, 128), F32), V((4, 8, 128), F32),
        V((NS, w, HID), F32), V((NS, h, HID), F32), V((NS, 8, h, 128), F32), V((16, 192, 128), F32),
    ]
    two = lambda *s: [dma(s), dma(s)]
    sems = [dma((6,))] + two(2, 2, 16) + two(Q, 2) + two(Q, 2) + two(NS, 2) + two(NS, 2)
    sems += two(1) + two(8) + two(4) + two(4) + two(4) + two(4) + two(4) + two(4)
    sems += two(NS) + two(NS, 8) + two(NS, 4) + two(NS, 4) + two(NS)
    loss, gi, go = pl.pallas_call(
        kernel,
        out_shape=(
            jax.ShapeDtypeStruct((1, 1), F32),
            jax.ShapeDtypeStruct((16, HID), F32),
            jax.ShapeDtypeStruct((64, D), F32),
        ),
        in_specs=[hb, hb, hb, vm, vm, vm, vm, vm],
        out_specs=(vm, vm, vm),
        scratch_shapes=scratch + sems,
        compiler_params=pltpu.CompilerParams(collective_id=0, has_side_effects=True, vmem_limit_bytes=58 << 20),
        cost_estimate=pl.CostEstimate(flops=12_000_000_000, bytes_accessed=17_000_000, transcendentals=2_000_000),
        name="feature_match",
    )(images, frequencies, gen_out, labels.reshape(1, NI), gen_labels.reshape(1, N), privacy_noise, latents, gen_in)
    return loss.reshape(()), gi, go


def solution(mesh):
    return jax.shard_map(
        per_device,
        mesh=mesh,
        in_specs=(
            P("dp", None),
            P("dp"),
            P(None, "feat"),
            P(None, None, "feat"),
            P("dp", None),
            P("dp"),
            P(),
            P(),
        ),
        out_specs=(P(), P("dp", None), P("dp", None)),
        check_vma=False,
    )
```

```python
import functools

import jax
import jax.numpy as jnp
from jax import lax
from jax.experimental import pallas as pl
from jax.experimental.pallas import tpu as pltpu
from jax.sharding import PartitionSpec as P

MESH = pl.DeviceIdType.MESH
F32 = jnp.float32
BF16 = jnp.bfloat16

SIN = (6.28318284102346, -41.34142273936724, 81.59620932441723, -76.58030929887768, 41.20616782312917, -12.272323133322006)
COS = (0.999999989172567, -19.73920453212146, 64.93911898457917, -85.45016555726593, 60.16783176141255, -25.968313346422505, 6.5296104065360066)

N, D, FL, HID, Z, NI = 256, 3072, 1024, 1024, 256, 384
ROWS = N + NI
SUBS = (80, 32, 48, 32)
STARTS = (0, 80, 112, 160)
FIRST = ('x', 'z', 'x', 'x')
REL = (2, 1, 3, 0)
NS = len(SUBS)
D_OWN = sum(SUBS)
Q = 4 * NS
ORDER = (
    ("A", 0, 0), ("A", 0, 1), ("I", 2, 0), ("I", 2, 1), ("I", 2, 2), ("I", 2, 3), ("I", 3, 0), ("I", 3, 1),
    ("A", 0, 2), ("K", 0), ("A", 0, 3), ("A", 1, 0), ("A", 1, 1), ("A", 1, 2), ("K", 1), ("B", 0, 0), ("A", 1, 3),
    ("I", 3, 2), ("I", 3, 3), ("B", 0, 1), ("K", 2), ("A", 2, 0), ("B", 1, 0), ("A", 2, 1), ("A", 2, 2), ("A", 2, 3),
    ("A", 3, 0), ("A", 3, 1), ("K", 3), ("B", 0, 2), ("B", 1, 1), ("B", 1, 2), ("B", 0, 3), ("A", 3, 2), ("A", 3, 3),
    ("G1",), ("B", 2, 0), ("B", 2, 1), ("B", 1, 3), ("B", 2, 2), ("B", 2, 3), ("B", 3, 0), ("B", 3, 1), ("D", 0),
    ("D", 1), ("B", 3, 2), ("B", 3, 3), ("O1", 0), ("O1", 1), ("G2",), ("D", 2), ("O1", 2), ("D", 3), ("O2", 0),
    ("G3",), ("O2", 1), ("O1", 3), ("O2", 2), ("O2", 3), ("O3", 0), ("G4",), ("O3", 1), ("O3", 2), ("O3", 3), ("G5",),
    ("O4", 0), ("O4", 1), ("O4", 2), ("O4", 3), ("G6",),
)
NT = (((1,), (1,)), ((), ()))


def poly(coeffs, u):
    r = coeffs[-1] * u + coeffs[-2]
    for c in coeffs[-3::-1]:
        r = r * u + c
    return r


def cos_sin(phase):
    t = phase * 0.15915494309189535
    f = t - jnp.round(t)
    u = f * f
    return poly(COS, u), f * poly(SIN, u)


def split(v):
    hi = v.astype(BF16)
    return hi, (v - hi.astype(F32)).astype(BF16)


def mm(a, b):
    return jnp.dot(a, b, preferred_element_type=F32)


def mmt(a, b):
    return lax.dot_general(a, b, NT, preferred_element_type=F32)


def kernel(images_h, freq_h, gen_out_h, noise_h, lat_h, gin_h, lab_ref, glab_ref,
           loss_ref, gi_ref, go_ref,
           freq, gout, lhs, noise3, lat, gin_w, noise, hidden, q_s, qt, s_s, st, latt, oneh, onet, cosg, sing, gp, rsb, gapb, pg, ph,
           part, ohi, olo, gin, xa, xb, zr, gic, gid, gix, giz, gig, lvx, lvz, gt_p, goc, god, gfull,
           lsem, send, ar_r, xa_r, xb_r, zr_r, g_r, o_r):
    dp = lax.axis_index("dp")
    ft = lax.axis_index("feat")
    core = lax.rem(dp, 2)
    chip = dp // 2
    x = ft // 4
    zh = lax.rem(ft, 4)

    def xdev(k):
        return (dp, lax.rem(x + k, 4) * 4 + zh)

    def zdev(k):
        return (dp, x * 4 + lax.rem(zh + k, 4))

    def cdev(k):
        return (lax.rem(chip + k, 8) * 2 + core, ft)

    other = (chip * 2 + 1 - core, ft)

    def put(group, src, dst, rs, dev):
        pltpu.make_async_remote_copy(
            src_ref=src, dst_ref=dst, send_sem=send.at[group], recv_sem=rs, device_id=dev, device_id_type=MESH
        ).start()

    def arrived(ref, rs):
        pltpu.make_async_copy(ref, ref, rs).wait()

    loads = [pltpu.make_async_copy(gen_out_h.at[:, pl.ds(n * 512, 512)], gout.at[:, pl.ds(n * 512, 512)], lsem.at[n]) for n in range(6)]
    loads.append(pltpu.make_async_copy(images_h, lhs.at[pl.ds(N, NI)], lsem.at[6]))
    for n in range(4):
        loads.append(pltpu.make_async_copy(freq_h.at[:, pl.ds(n * 256, 256)], freq.at[:, pl.ds(n * 256, 256)], lsem.at[7 + n]))
    loads.append(pltpu.make_async_copy(lat_h, lat, lsem.at[11]))
    loads.append(pltpu.make_async_copy(gin_h, gin_w, lsem.at[12]))
    loads.append(pltpu.make_async_copy(noise_h, noise3, lsem.at[13]))
    loads[11].start()
    loads[12].start()
    for n in range(6):
        loads[n].start()
    loads[13].start()

    bar = pltpu.get_barrier_semaphore()

    def greet_dp(k, carry):
        pl.semaphore_signal(bar, inc=1, device_id=(lax.rem(dp + k, 16), ft), device_id_type=MESH)
        return carry

    lax.fori_loop(1, 16, greet_dp, 0)
    for k in (1, 2, 3):
        pl.semaphore_signal(bar, inc=1, device_id=xdev(k), device_id_type=MESH)
        pl.semaphore_signal(bar, inc=1, device_id=zdev(k), device_id_type=MESH)

    cls = lax.broadcasted_iota(jnp.int32, (32, N), 0)
    on_g = (jnp.where(cls < 16, cls, cls - 16) == glab_ref[...][None, :]).astype(F32)
    cls_g = lax.broadcasted_iota(jnp.int32, (16, N), 0)
    oneh[0:16, 0:N] = (cls_g == glab_ref[...][None, :]).astype(F32).astype(BF16)
    oneh[16:32, 0:N] = jnp.zeros((16, N), BF16)
    cls_d = lax.broadcasted_iota(jnp.int32, (16, NI), 0)
    oneh[0:16, N:ROWS] = jnp.zeros((16, NI), BF16)
    oneh[16:32, N:ROWS] = (cls_d == lab_ref[...][None, :]).astype(F32).astype(BF16)
    onet[...] = jnp.concatenate([on_g, jnp.zeros((96, N), F32)], axis=0).T.astype(BF16)
    loads[11].wait()
    latt[...] = lat[...].astype(F32).T.astype(BF16)
    loads[12].wait()

    pre = mm(lat[...], gin_w[...])
    sig = jax.nn.sigmoid(pre)
    hidden[...] = (pre * sig).astype(BF16)
    s_s[...] = sig * (1.0 + pre * (1.0 - sig))

    for n in range(6):
        loads[n].wait()
        if n < 5:
            loads[6 + n].start()
        cols = slice(n * 512, n * 512 + 512)
        out = jnp.tanh(mm(hidden[...], gout[:, cols]))
        lhs[0:N, cols] = out.astype(BF16)
        q_s[:, cols] = 1.0 - out * out
    loads[6].wait()

    def phase(n):
        loads[7 + n].wait()
        ph[n % 2] = mm(lhs[...], freq[:, n * 256 : n * 256 + 256])

    def sums(n):
        cols = slice(n * 256, n * 256 + 256)
        cs, sn = cos_sin(ph[n % 2])
        cosg[:, cols] = cs[0:N]
        sing[:, cols] = sn[0:N]
        for k, v in ((0, cs), (1, sn)):
            hi, lo = split(v)
            total = mm(oneh[...], hi) + mm(oneh[...], lo)
            gp[16 * k : 16 * k + 16, cols] = total[0:16] * (10.0 / 4096.0) - total[16:32] * (10.0 / 6144.0)

    def block(o):
        return pl.multiple_of(8 * (o // 4), 8), pl.multiple_of(128 * lax.rem(o, 4), 128)

    row_me, lane_me = block(dp)

    def ar_send(h):
        rsb[h, dp] = gp[pl.ds(row_me, 8), pl.ds(pl.multiple_of(h * 512 + lane_me, 128), 128)]

        def go(k, carry):
            peer = lax.rem(dp + k, 16)
            r, l = block(peer)
            put(0, gp.at[pl.ds(r, 8), pl.ds(pl.multiple_of(h * 512 + l, 128), 128)], rsb.at[h, dp], ar_r.at[h, 0], (peer, ft))
            return carry

        lax.fori_loop(1, 16, go, 0)

    def ar_spread(h):
        arrived(rsb.at[h, pl.ds(0, 15)], ar_r.at[h, 0])
        mine = gapb.at[h, pl.ds(row_me, 8), pl.ds(lane_me, 128)]
        mine[...] = jnp.sum(rsb[h], axis=0)

        def go(k, carry):
            put(0, mine, mine, ar_r.at[h, 1], (lax.rem(dp + k, 16), ft))
            return carry

        lax.fori_loop(1, 16, go, 0)

    def gap(h):
        arrived(rsb.at[h, pl.ds(0, 15)], ar_r.at[h, 1])
        cols = slice(h * 512, h * 512 + 512)
        g = gapb[h] - noise[:, cols]
        sq = g * g
        lv = sq[0:8] + sq[8:16] + sq[16:24] + sq[24:32]
        lv = lv[:, 0:128] + lv[:, 128:256] + lv[:, 256:384] + lv[:, 384:512]
        hi, lo = split(g * (160.0 / 4096.0))
        g0 = mm(onet[:, 0:32], jnp.concatenate([hi[0:16], lo[0:16]], axis=0))
        g1 = mm(onet[:, 0:32], jnp.concatenate([hi[16:32], lo[16:32]], axis=0))
        pg[:, cols] = (cosg[:, cols] * g1 - sing[:, cols] * g0).astype(BF16)
        return lv

    phase(0)
    phase(1)
    sums(0)
    phase(2)
    sums(1)
    pl.semaphore_wait(bar, 21)
    ar_send(0)
    phase(3)
    sums(2)
    ar_spread(0)
    sums(3)
    ar_send(1)

    def turn_q(n, carry):
        o = pl.multiple_of(n * 256, 256)
        qt[pl.ds(o, 256), :] = q_s[:, pl.ds(o, 256)].T
        return carry

    lax.fori_loop(0, 12, turn_q, 0)
    loads[13].wait()
    noise[...] = jnp.zeros_like(noise)
    for k in range(2):
        noise[16 * k : 16 * k + 10, :] = noise3[:, k, :]
    lv = gap(0)

    def first_half(n, carry):
        rows = pl.ds(pl.multiple_of(n * 768, 256), 768)
        part[rows, :] = mmt(freq[rows, 0:512], pg[:, 0:512])
        return carry

    lax.fori_loop(0, 4, first_half, 0)
    ar_spread(1)

    def turn_s(n, carry):
        o = pl.multiple_of(n * 256, 256)
        st[pl.ds(o, 256), :] = s_s[:, pl.ds(o, 256)].T
        return carry

    lax.fori_loop(0, 4, turn_s, 0)
    lv = lv + gap(1)

    def rows_at(r1, r2, s, half, rows):
        xr, zr = (r1, r2) if FIRST[s] == "x" else (r2, r1)
        base = lax.rem(x + xr, 4) * 768 + lax.rem(zh + zr, 4) * 192 + STARTS[s] + half
        return part.at[pl.ds(pl.multiple_of(base, 8), rows), :]

    def dev1(s, k):
        return xdev(k) if FIRST[s] == "x" else zdev(k)

    def dev2(s, k):
        return zdev(k) if FIRST[s] == "x" else xdev(k)

    def second_half(xr):
        rows = pl.ds(pl.multiple_of(lax.rem(x + xr, 4) * 768, 256), 768)
        part[rows, :] += mmt(freq[rows, 512:1024], pg[:, 512:1024])

    def do_i(s, k):
        h, q = SUBS[s] // 2, s * 4 + k
        for b in range(2):
            put(1, rows_at(2, REL[k], s, b * h, h), xa.at[q, b, pl.ds(0, h)], xa_r.at[q], dev1(s, (1, 3)[b]))

    def do_a(s, k):
        w, q = SUBS[s], s * 4 + k
        h = w // 2
        arrived(xa.at[q, :, pl.ds(0, h)], xa_r.at[q])
        for b in range(2):
            r = rows_at((1, 3)[b], REL[k], s, b * h, h)
            r[...] = r[...] + xa[q, b, 0:h]
            put(1, rows_at((1, 3)[b], REL[k], s, 0, w), xb.at[q, b, pl.ds(0, w)], xb_r.at[q], dev1(s, (1, 3)[b]))

    def do_b(s, k):
        w, q = SUBS[s], s * 4 + k
        arrived(xb.at[q, :, pl.ds(0, w)], xb_r.at[q])
        r = rows_at(0, REL[k], s, 0, w)
        r[...] = r[...] + xb[q, 0, 0:w] + xb[q, 1, 0:w]
        if k < 3:
            put(1, r, zr.at[s, k, pl.ds(0, w)], zr_r.at[s], dev2(s, REL[k]))

    def do_d(s):
        w = SUBS[s]
        arrived(zr.at[s, :, pl.ds(0, w)], zr_r.at[s])
        own = rows_at(0, 0, s, 0, w)[...] + zr[s, 0, 0:w] + zr[s, 1, 0:w] + zr[s, 2, 0:w]
        base = pl.multiple_of(ft * 192 + STARTS[s], 8)
        og = (own * qt[pl.ds(base, w), :]).astype(BF16)
        gt_p[s, 0:w, :] = mm(og, hidden[...])
        h = w // 2
        put(2, gt_p.at[s, pl.ds(pl.multiple_of((1 - core) * h, 8), h)], goc.at[s, pl.ds(0, h)], o_r.at[s, 0], other)

    second_half(2)
    for s in range(NS):
        if FIRST[s] == "x" and s < 1:
            for k in range(4):
                do_i(s, k)

    lvx[x] = lv
    for k in (1, 3, 2):
        put(3, lvx.at[x], lvx.at[x], g_r.at[6], xdev(k))

    for xr in (1, 3, 0):
        second_half(xr)
    for s in range(NS):
        if FIRST[s] == "z":
            for k in range(4):
                do_i(s, k)

    def factor(n, carry):
        rows = pl.ds(pl.multiple_of(n * 256, 256), 256)
        hi, lo = split(part[rows, :] * qt[rows, :])
        ohi[rows, :] = hi
        olo[rows, :] = lo
        return carry

    lax.fori_loop(0, 12, factor, 0)

    def rows_of(s, c):
        h = SUBS[s] // 2
        return pl.ds(pl.multiple_of(STARTS[s] + c * h, 8), h)

    def go1(s):
        h = SUBS[s] // 2
        mine = pl.ds(pl.multiple_of(core * h, 8), h)
        arrived(goc.at[s, pl.ds(0, h)], o_r.at[s, 0])
        r = gt_p.at[s, mine]
        r[...] = r[...] + goc[s, 0:h]
        for k in range(1, 8):
            peer = lax.rem(chip + k, 8)
            put(2, gt_p.at[s, mine, pl.ds(pl.multiple_of(peer * 128, 128), 128)], god.at[s, chip, pl.ds(0, h)], o_r.at[s, 1], cdev(k))
        god[s, chip, 0:h] = gt_p[s, mine, pl.ds(pl.multiple_of(chip * 128, 128), 128)]

    def go2(s):
        h = SUBS[s] // 2
        arrived(god.at[s, pl.ds(0, 7), pl.ds(0, h)], o_r.at[s, 1])
        gfull[ft, rows_of(s, core), :] = jnp.sum(god[s, :, 0:h], axis=0)
        at = gfull.at[ft, rows_of(s, core), :]
        for k in (1, 3, 2):
            put(2, at, at, o_r.at[s, 2], zdev(k))

    def go3(s):
        h = SUBS[s] // 2
        arrived(god.at[s, pl.ds(0, 3), pl.ds(0, h)], o_r.at[s, 2])
        at = gfull.at[pl.ds(x * 4, 4), rows_of(s, core), :]
        for k in (1, 3, 2):
            put(2, at, at, o_r.at[s, 3], xdev(k))

    def go4(s):
        arrived(gfull.at[pl.ds(0, 12), rows_of(s, core), :], o_r.at[s, 3])
        at = gfull.at[:, rows_of(s, core), :]
        put(2, at, at, o_r.at[s, 4], other)

    def back(n):
        rows = slice(n * 256, n * 256 + 256)
        bh = mm(gout[rows, :], ohi[...]) + mm(gout[rows, :], olo[...])
        hi, lo = split(bh * st[rows, :])
        g = mmt(latt[...], hi) + mmt(latt[...], lo)
        gin[:, :, :, rows] = g.reshape(8, 2, 16, 256)
        if n == 3:
            put(3, gin.at[:, 1 - core], gic, g_r.at[0], other)

    def gi1():
        arrived(gic, g_r.at[0])
        gin[:, core] = gin[:, core] + gic[...]
        for k in range(1, 8):
            put(3, gin.at[lax.rem(chip + k, 8), core], gid.at[chip], g_r.at[1], cdev(k))
        gid[chip] = gin[chip, core]

    def gi2():
        arrived(gid.at[pl.ds(0, 7)], g_r.at[1])
        gsum = jnp.sum(gid[...], axis=0)
        gic[0] = gsum
        for k in (1, 3, 2):
            cols = pl.ds(pl.multiple_of(lax.rem(x + k, 4) * 256, 256), 256)
            put(3, gic.at[0, :, cols], gix.at[x], g_r.at[2], xdev(k))
        gix[x] = gic[0, :, pl.ds(pl.multiple_of(x * 256, 256), 256)]
        arrived(lvx.at[pl.ds(0, 3)], g_r.at[6])
        lvz[zh] = jnp.sum(lvx[...], axis=0)
        for k in (1, 3, 2):
            put(3, lvz.at[zh], lvz.at[zh], g_r.at[7], zdev(k))

    def zblock(p):
        return pl.ds(pl.multiple_of(8 * (p // 2), 8), 8), pl.ds(pl.multiple_of(128 * lax.rem(p, 2), 128), 128)

    def gi3():
        arrived(gix.at[pl.ds(0, 3)], g_r.at[2])
        gic[1, :, 0:256] = jnp.sum(gix[...], axis=0)
        for k in (1, 3, 2):
            r, l = zblock(lax.rem(zh + k, 4))
            put(3, gic.at[1, r, l], giz.at[zh], g_r.at[3], zdev(k))
        r, l = zblock(zh)
        giz[zh] = gic[1, r, l]

    def gi4():
        arrived(giz.at[pl.ds(0, 3)], g_r.at[3])
        r, l = zblock(zh)
        gig[x, r, l] = jnp.sum(giz[...], axis=0)
        for k in (1, 3, 2):
            put(3, gig.at[x, r, l], gig.at[x, r, l], g_r.at[4], zdev(k))

    def gi5():
        arrived(giz.at[pl.ds(0, 3)], g_r.at[4])
        for k in (1, 3, 2):
            put(3, gig.at[x], gig.at[x], g_r.at[5], xdev(k))

    def gi6():
        arrived(gix.at[pl.ds(0, 3)], g_r.at[5])
        for p in range(4):
            gi_ref[:, p * 256 : p * 256 + 256] = gig[p]
        arrived(lvz.at[pl.ds(0, 3)], g_r.at[7])
        loss_ref[...] = jnp.sum(jnp.sum(lvz[...], axis=0), axis=(0, 1), keepdims=True) * (1.0 / 32768.0)

    steps = {"I": do_i, "A": do_a, "B": do_b, "D": do_d, "O1": go1, "O2": go2, "O3": go3, "O4": go4,
             "K": back, "G1": gi1, "G2": gi2, "G3": gi3, "G4": gi4, "G5": gi5, "G6": gi6}
    for name, *where in ORDER:
        steps[name](*where)
    for s in range(NS):
        arrived(gfull.at[:, rows_of(s, 1 - core), :], o_r.at[s, 4])

    def turn(p, carry):
        v = gfull[pl.ds(p * 2, 2)].reshape(384, 128).T
        go_ref[:, pl.ds(pl.multiple_of(p * 384, 128), 384)] = jnp.where(core == 0, v[0:64], v[64:128])
        return carry

    lax.fori_loop(0, 8, turn, 0)
    for group, rows in enumerate((240, 15 * D_OWN, 23 * D_OWN // 2, 1104)):
        arrived(part.at[pl.ds(0, rows)], send.at[group])


def hand_on(a, b, c, ao, bo, co):
    ao[...] = a[...]
    bo[...] = b[...]
    co[...] = c[...]


def per_device(images, labels, frequencies, privacy_noise, latents, gen_labels, gen_in, gen_out):
    vm = pl.BlockSpec(memory_space=pltpu.VMEM)
    hb = pl.BlockSpec(memory_space=pltpu.HBM)
    V = pltpu.VMEM
    dma = pltpu.SemaphoreType.DMA
    w = max(SUBS)
    h = w // 2
    scratch = [
        V((D, FL), BF16), V((HID, D), BF16), V((ROWS, D), BF16), V((10, 2, FL), F32), V((N, Z), BF16), V((Z, HID), BF16), V((32, FL), F32), V((N, HID), BF16),
        V((N, D), F32), V((D, N), F32), V((N, HID), F32), V((HID, N), F32), V((Z, N), BF16),
        V((32, ROWS), BF16), V((N, 128), BF16), V((N, FL), F32), V((N, FL), F32), V((32, FL), F32),
        V((2, 16, 8, 128), F32), V((2, 32, 512), F32), V((N, FL), BF16), V((2, ROWS, 256), F32),
        V((D, N), F32), V((D, N), BF16), V((D, N), BF16), V((8, 2, 16, HID), F32),
        V((Q, 2, h, N), F32), V((Q, 2, w, N), F32), V((NS, 3, w, N), F32),
        V((8, 16, HID), F32), V((8, 16, HID), F32), V((4, 16, 256), F32), V((4, 8, 128), F32), V((4, 16, 256), F32),
        V((4, 8, 128), F32), V((4, 8, 128), F32),
        V((NS, w, HID), F32), V((NS, h, HID), F32), V((NS, 8, h, 128), F32), V((16, 192, 128), F32),
    ]
    sems = [dma((14,)), dma((4,)), dma((2, 2)), dma((Q,)), dma((Q,)), dma((NS,)), dma((8,)), dma((NS, 5))]
    loss, gi, go = pl.pallas_call(
        kernel,
        out_shape=(
            jax.ShapeDtypeStruct((1, 1), F32),
            jax.ShapeDtypeStruct((16, HID), F32),
            jax.ShapeDtypeStruct((64, D), F32),
        ),
        in_specs=[hb] * 6 + [vm] * 2,
        out_specs=(vm, vm, vm),
        scratch_shapes=scratch + sems,
        compiler_params=pltpu.CompilerParams(collective_id=0, has_side_effects=True, vmem_limit_bytes=58 << 20),
        cost_estimate=pl.CostEstimate(flops=12_000_000_000, bytes_accessed=17_000_000, transcendentals=2_000_000),
        name="feature_match",
    )(images, frequencies, gen_out, privacy_noise, latents, gen_in, labels, gen_labels)
    loss, gi, go = pl.pallas_call(
        hand_on,
        out_shape=(
            jax.ShapeDtypeStruct((1, 1), F32),
            jax.ShapeDtypeStruct((16, HID), F32),
            jax.ShapeDtypeStruct((64, D), F32),
        ),
        in_specs=[vm] * 3,
        out_specs=(vm,) * 3,
        name="hand_on",
    )(loss, gi, go)
    return loss.reshape(()), gi, go


def solution(mesh):
    return jax.shard_map(
        per_device,
        mesh=mesh,
        in_specs=(
            P("dp", None),
            P("dp"),
            P(None, "feat"),
            P(None, None, "feat"),
            P("dp", None),
            P("dp"),
            P(),
            P(),
        ),
        out_specs=(P(), P("dp", None), P("dp", None)),
        check_vma=False,
    )
```

```python
import functools

import jax
import jax.numpy as jnp
from jax import lax
from jax.experimental import pallas as pl
from jax.experimental.pallas import tpu as pltpu
from jax.sharding import PartitionSpec as P

MESH = pl.DeviceIdType.MESH
F32 = jnp.float32
BF16 = jnp.bfloat16

SIN = (6.28318284102346, -41.34142273936724, 81.59620932441723, -76.58030929887768, 41.20616782312917, -12.272323133322006)
COS = (0.999999989172567, -19.73920453212146, 64.93911898457917, -85.45016555726593, 60.16783176141255, -25.968313346422505, 6.5296104065360066)

N, D, FL, HID, Z, NI = 256, 3072, 1024, 1024, 256, 384
ROWS = N + NI
SUBS = (64, 32, 64, 32)
STARTS = (0, 64, 96, 160)
FIRST = ('x', 'z', 'x', 'x')
REL = (2, 1, 3, 0)
NS = len(SUBS)
D_OWN = sum(SUBS)
Q = 4 * NS
ORDER = (
    ("A", 0, 0), ("A", 0, 1), ("I", 2, 0), ("I", 2, 1), ("A", 0, 2), ("I", 2, 2), ("K", 0), ("A", 0, 3), ("A", 1, 0),
    ("K", 1), ("A", 1, 1), ("A", 1, 2), ("I", 2, 3), ("I", 3, 0), ("B", 0, 0), ("A", 1, 3), ("I", 3, 1), ("I", 3, 2),
    ("I", 3, 3), ("K", 2), ("B", 0, 1), ("A", 2, 0), ("K", 3), ("B", 1, 0), ("A", 2, 1), ("B", 0, 2), ("B", 1, 1),
    ("A", 2, 2), ("G1",), ("B", 0, 3), ("B", 1, 2), ("A", 2, 3), ("A", 3, 0), ("A", 3, 1), ("A", 3, 2), ("A", 3, 3),
    ("B", 2, 0), ("B", 1, 3), ("B", 2, 1), ("D", 0), ("B", 2, 2), ("D", 1), ("O1", 0), ("B", 2, 3), ("B", 3, 0),
    ("O1", 1), ("B", 3, 1), ("G1b",), ("B", 3, 2), ("B", 3, 3), ("D", 2), ("O1b", 0), ("O1", 2), ("O1b", 1), ("G2",),
    ("O2", 0), ("D", 3), ("O2", 1), ("O1", 3), ("O1b", 2), ("O3", 0), ("O2", 2), ("O3", 1), ("G3",), ("O2", 3),
    ("O4", 0), ("O3", 2), ("O4", 1), ("G4",), ("O4", 3), ("O4", 2),
)
NT = (((1,), (1,)), ((), ()))


def poly(coeffs, u):
    r = coeffs[-1] * u + coeffs[-2]
    for c in coeffs[-3::-1]:
        r = r * u + c
    return r


def cos_sin(phase):
    t = phase * 0.15915494309189535
    f = t - jnp.round(t)
    u = f * f
    return poly(COS, u), f * poly(SIN, u)


def split(v):
    hi = v.astype(BF16)
    return hi, (v - hi.astype(F32)).astype(BF16)


def mm(a, b):
    return jnp.dot(a, b, preferred_element_type=F32)


def mmt(a, b):
    return lax.dot_general(a, b, NT, preferred_element_type=F32)


def kernel(images_h, freq_h, gen_out_h, noise_h, lat_h, gin_h, lab_ref, glab_ref,
           loss_ref, gi_ref, go_ref,
           freq, gout, lhs, noise3, lat, gin_w, noise, hidden, q_s, qt, s_s, st, latt, oneh, onet, cosg, sing, gp, from_core0, from_core1, chips0, chips1, gap0, gap1, pg, ph,
           part, ohi, gin, xa, xb, zr, gic, gid, gio, gix, gig, lvx, gt_p, goc, god, goy, goz, gfull,
           lsem, send, ar_r, xa_r, xb_r, zr_r, g_r, o_r):
    dp = lax.axis_index("dp")
    ft = lax.axis_index("feat")
    core = lax.rem(dp, 2)
    chip = dp // 2
    x = ft // 4
    zh = lax.rem(ft, 4)

    def xdev(k):
        return (dp, lax.rem(x + k, 4) * 4 + zh)

    def zdev(k):
        return (dp, x * 4 + lax.rem(zh + k, 4))

    def cdev(k):
        return (lax.rem(chip + k, 8) * 2 + core, ft)

    other = (chip * 2 + 1 - core, ft)
    zl = chip // 4
    y = lax.rem(chip, 4)

    def ydev(k):
        return ((zl * 4 + lax.rem(y + k, 4)) * 2 + core, ft)

    zldev = (((1 - zl) * 4 + y) * 2 + core, ft)

    def put(group, src, dst, rs, dev):
        pltpu.make_async_remote_copy(
            src_ref=src, dst_ref=dst, send_sem=send.at[group], recv_sem=rs, device_id=dev, device_id_type=MESH
        ).start()

    def arrived(ref, rs):
        pltpu.make_async_copy(ref, ref, rs).wait()

    loads = [pltpu.make_async_copy(gen_out_h.at[:, pl.ds(n * 512, 512)], gout.at[:, pl.ds(n * 512, 512)], lsem.at[n]) for n in range(6)]
    loads.append(pltpu.make_async_copy(images_h, lhs.at[pl.ds(N, NI)], lsem.at[6]))
    for n in range(4):
        loads.append(pltpu.make_async_copy(freq_h.at[:, pl.ds(n * 256, 256)], freq.at[:, pl.ds(n * 256, 256)], lsem.at[7 + n]))
    loads.append(pltpu.make_async_copy(lat_h, lat, lsem.at[11]))
    loads.append(pltpu.make_async_copy(gin_h, gin_w, lsem.at[12]))
    loads.append(pltpu.make_async_copy(noise_h, noise3, lsem.at[13]))
    loads[11].start()
    loads[12].start()
    for n in range(6):
        loads[n].start()
    loads[13].start()

    bar = pltpu.get_barrier_semaphore()

    def greet(k, carry):
        pl.semaphore_signal(bar, inc=1, device_id=(lax.rem(dp + k, 16), ft), device_id_type=MESH)
        pl.semaphore_signal(bar, inc=1, device_id=(dp, lax.rem(ft + k, 16)), device_id_type=MESH)
        return carry

    lax.fori_loop(1, 16, greet, 0)

    cls = lax.broadcasted_iota(jnp.int32, (32, N), 0)
    on_g = (jnp.where(cls < 16, cls, cls - 16) == glab_ref[...][None, :]).astype(F32)
    cls_g = lax.broadcasted_iota(jnp.int32, (16, N), 0)
    oneh[0:16, 0:N] = (cls_g == glab_ref[...][None, :]).astype(F32).astype(BF16)
    oneh[16:32, 0:N] = jnp.zeros((16, N), BF16)
    cls_d = lax.broadcasted_iota(jnp.int32, (16, NI), 0)
    oneh[0:16, N:ROWS] = jnp.zeros((16, NI), BF16)
    oneh[16:32, N:ROWS] = (cls_d == lab_ref[...][None, :]).astype(F32).astype(BF16)
    onet[...] = jnp.concatenate([on_g, jnp.zeros((96, N), F32)], axis=0).T.astype(BF16)
    loads[11].wait()
    latt[...] = lat[...].astype(F32).T.astype(BF16)
    loads[12].wait()

    pre = mm(lat[...], gin_w[...])
    sig = jax.nn.sigmoid(pre)
    hidden[...] = (pre * sig).astype(BF16)
    s_s[...] = sig * (1.0 + pre * (1.0 - sig))

    for n in range(6):
        loads[n].wait()
        if n < 5:
            loads[6 + n].start()
        cols = slice(n * 512, n * 512 + 512)
        out = jnp.tanh(mm(hidden[...], gout[:, cols]))
        lhs[0:N, cols] = out.astype(BF16)
        q_s[:, cols] = 1.0 - out * out
    loads[6].wait()

    def phase(n):
        loads[7 + n].wait()
        ph[n % 2] = mm(lhs[...], freq[:, n * 256 : n * 256 + 256])

    def sums(n):
        cols = slice(n * 256, n * 256 + 256)
        cs, sn = cos_sin(ph[n % 2])
        cosg[:, cols] = cs[0:N]
        sing[:, cols] = sn[0:N]
        for k, v in ((0, cs), (1, sn)):
            hi, lo = split(v)
            total = mm(oneh[...], hi) + mm(oneh[...], lo)
            gp[16 * k : 16 * k + 16, cols] = total[0:16] * (10.0 / 4096.0) - total[16:32] * (10.0 / 6144.0)

    parts = ((slice(0, 512), from_core0, chips0, gap0), (slice(512, 1024), from_core1, chips1, gap1))
    own_rows = pl.ds(pl.multiple_of(16 * core, 16), 16)
    other_rows = pl.ds(pl.multiple_of(16 * (1 - core), 16), 16)

    def ar1(h):
        cols, got, _, _ = parts[h]
        put(0, gp.at[other_rows, cols], got, ar_r.at[h, 0], other)

    def ar2(h):
        cols, got, chips, _ = parts[h]
        arrived(got, ar_r.at[h, 0])
        chips[chip] = gp[own_rows, cols] + got[...]
        for k in range(1, 8):
            put(0, chips.at[chip], chips.at[chip], ar_r.at[h, 1], cdev(k))

    def ar3(h):
        _, _, chips, whole = parts[h]
        arrived(chips.at[pl.ds(0, 7)], ar_r.at[h, 1])
        whole[own_rows, :] = jnp.sum(chips[...], axis=0)
        put(0, whole.at[own_rows], whole.at[own_rows], ar_r.at[h, 2], other)

    def gap(h):
        cols, _, _, whole = parts[h]
        arrived(whole.at[other_rows], ar_r.at[h, 2])
        g = whole[...] - noise[:, cols]
        sq = g * g
        lv = sq[0:8] + sq[8:16] + sq[16:24] + sq[24:32]
        lv = sum(lv[:, i : i + 128] for i in range(0, lv.shape[1], 128))
        hi, lo = split(g * (160.0 / 4096.0))
        g0 = mm(onet[:, 0:32], jnp.concatenate([hi[0:16], lo[0:16]], axis=0))
        g1 = mm(onet[:, 0:32], jnp.concatenate([hi[16:32], lo[16:32]], axis=0))
        pg[:, cols] = (cosg[:, cols] * g1 - sing[:, cols] * g0).astype(BF16)
        return lv

    phase(0)
    phase(1)
    sums(0)
    phase(2)
    sums(1)
    pl.semaphore_wait(bar, 30)
    ar1(0)
    phase(3)
    sums(2)
    ar2(0)
    sums(3)
    ar1(1)
    ar2(1)

    def turn_q(n, carry):
        o = pl.multiple_of(n * 256, 256)
        qt[pl.ds(o, 256), :] = q_s[:, pl.ds(o, 256)].T
        return carry

    lax.fori_loop(0, 12, turn_q, 0)
    ar3(0)
    loads[13].wait()
    noise[...] = jnp.zeros_like(noise)
    for k in range(2):
        noise[16 * k : 16 * k + 10, :] = noise3[:, k, :]

    def turn_s(n, carry):
        o = pl.multiple_of(n * 256, 256)
        st[pl.ds(o, 256), :] = s_s[:, pl.ds(o, 256)].T
        return carry

    lax.fori_loop(0, 4, turn_s, 0)
    lv = gap(0)

    ar3(1)

    def first_half(n, carry):
        rows = pl.ds(pl.multiple_of(n * 768, 256), 768)
        part[rows, :] = mmt(freq[rows, 0:512], pg[:, 0:512])
        return carry

    lax.fori_loop(0, 4, first_half, 0)

    lv = lv + gap(1)

    def rows_at(r1, r2, s, half, rows):
        xr, zr = (r1, r2) if FIRST[s] == "x" else (r2, r1)
        base = lax.rem(x + xr, 4) * 768 + lax.rem(zh + zr, 4) * 192 + STARTS[s] + half
        return part.at[pl.ds(pl.multiple_of(base, 8), rows), :]

    def dev1(s, k):
        return xdev(k) if FIRST[s] == "x" else zdev(k)

    def dev2(s, k):
        return zdev(k) if FIRST[s] == "x" else xdev(k)

    def second_half(xr):
        rows = pl.ds(pl.multiple_of(lax.rem(x + xr, 4) * 768, 256), 768)
        part[rows, :] += mmt(freq[rows, 512:1024], pg[:, 512:1024])

    def do_i(s, k):
        h, q = SUBS[s] // 2, s * 4 + k
        for b in range(2):
            put(1, rows_at(2, REL[k], s, b * h, h), xa.at[q, b, pl.ds(0, h)], xa_r.at[q], dev1(s, (1, 3)[b]))

    def do_a(s, k):
        w, q = SUBS[s], s * 4 + k
        h = w // 2
        arrived(xa.at[q, :, pl.ds(0, h)], xa_r.at[q])
        for b in range(2):
            r = rows_at((1, 3)[b], REL[k], s, b * h, h)
            r[...] = r[...] + xa[q, b, 0:h]
            put(1, rows_at((1, 3)[b], REL[k], s, 0, w), xb.at[q, b, pl.ds(0, w)], xb_r.at[q], dev1(s, (1, 3)[b]))

    def do_b(s, k):
        w, q = SUBS[s], s * 4 + k
        arrived(xb.at[q, :, pl.ds(0, w)], xb_r.at[q])
        r = rows_at(0, REL[k], s, 0, w)
        r[...] = r[...] + xb[q, 0, 0:w] + xb[q, 1, 0:w]
        if k < 3:
            put(1, r, zr.at[s, k, pl.ds(0, w)], zr_r.at[s], dev2(s, REL[k]))

    def do_d(s):
        w = SUBS[s]
        arrived(zr.at[s, :, pl.ds(0, w)], zr_r.at[s])
        own = rows_at(0, 0, s, 0, w)[...] + zr[s, 0, 0:w] + zr[s, 1, 0:w] + zr[s, 2, 0:w]
        base = pl.multiple_of(ft * 192 + STARTS[s], 8)
        og = (own * qt[pl.ds(base, w), :]).astype(BF16)
        gt_p[s, 0:w, :] = mm(og, hidden[...])
        h = w // 2
        put(2, gt_p.at[s, pl.ds(pl.multiple_of((1 - core) * h, 8), h)], goc.at[s, pl.ds(0, h)], o_r.at[s, 0], other)

    second_half(2)
    for s in range(NS):
        if FIRST[s] == "x" and s < 1:
            for k in range(4):
                do_i(s, k)

    lvx[ft] = lv
    def tell(k, carry):
        put(3, lvx.at[ft], lvx.at[ft], g_r.at[4], (dp, lax.rem(ft + k, 16)))
        return carry

    lax.fori_loop(1, 16, tell, 0)
    for xr in (1, 3, 0):
        second_half(xr)
    for s in range(NS):
        if FIRST[s] == "z":
            for k in range(4):
                do_i(s, k)

    def factor(n, carry):
        rows = pl.ds(pl.multiple_of(n * 256, 256), 256)
        ohi[rows, :] = (part[rows, :] * qt[rows, :]).astype(BF16)
        return carry

    lax.fori_loop(0, 12, factor, 0)

    def rows_of(s, c):
        h = SUBS[s] // 2
        return pl.ds(pl.multiple_of(STARTS[s] + c * h, 8), h)

    def go1(s):
        h = SUBS[s] // 2
        mine = pl.ds(pl.multiple_of(core * h, 8), h)
        arrived(goc.at[s, pl.ds(0, h)], o_r.at[s, 0])
        r = gt_p.at[s, mine]
        r[...] = r[...] + goc[s, 0:h]
        if s == NS - 1:
            for k in range(1, 8):
                peer = lax.rem(chip + k, 8)
                put(2, gt_p.at[s, mine, pl.ds(pl.multiple_of(peer * 128, 128), 128)], god.at[s, chip, pl.ds(0, h)], o_r.at[s, 1], cdev(k))
            god[s, chip, 0:h] = gt_p[s, mine, pl.ds(pl.multiple_of(chip * 128, 128), 128)]
            return
        for t in range(2):
            for k in (1, 3, 2):
                cols = pl.ds(pl.multiple_of((t * 4 + lax.rem(y + k, 4)) * 128, 128), 128)
                put(2, gt_p.at[s, mine, cols], god.at[s, t * 4 + y, pl.ds(0, h)], o_r.at[s, 1], ydev(k))
            god[s, t * 4 + y, 0:h] = gt_p[s, mine, pl.ds(pl.multiple_of((t * 4 + y) * 128, 128), 128)]

    def go1b(s):
        h = SUBS[s] // 2
        arrived(god.at[s, pl.ds(0, 6), pl.ds(0, h)], o_r.at[s, 1])
        for t in range(2):
            goy[s, t, 0:h] = jnp.sum(god[s, 4 * t : 4 * t + 4, 0:h], axis=0)
        put(2, goy.at[s, 1 - zl, pl.ds(0, h)], goz.at[s, pl.ds(0, h)], o_r.at[s, 5], zldev)

    def go2(s):
        h = SUBS[s] // 2
        if s == NS - 1:
            arrived(god.at[s, pl.ds(0, 7), pl.ds(0, h)], o_r.at[s, 1])
            gfull[ft, rows_of(s, core), :] = jnp.sum(god[s, :, 0:h], axis=0)
        else:
            arrived(goz.at[s, pl.ds(0, h)], o_r.at[s, 5])
            gfull[ft, rows_of(s, core), :] = goy[s, zl, 0:h] + goz[s, 0:h]
        at = gfull.at[ft, rows_of(s, core), :]
        if s < NS - 1:
            for k in (1, 3, 2):
                put(2, at, at, o_r.at[s, 2], zdev(k))
        else:

            def go(k, carry):
                put(2, at, at, o_r.at[s, 3], (dp, lax.rem(ft + k, 16)))
                return carry

            lax.fori_loop(1, 16, go, 0)

    def go3(s):
        h = SUBS[s] // 2
        arrived(god.at[s, pl.ds(0, 3), pl.ds(0, h)], o_r.at[s, 2])
        at = gfull.at[pl.ds(x * 4, 4), rows_of(s, core), :]
        for k in (1, 3, 2):
            put(2, at, at, o_r.at[s, 3], xdev(k))

    def go4(s):
        arrived(gfull.at[pl.ds(0, 12 if s < NS - 1 else 15), rows_of(s, core), :], o_r.at[s, 3])
        at = gfull.at[:, rows_of(s, core), :]
        put(2, at, at, o_r.at[s, 4], other)

    def back(n):
        rows = slice(n * 256, n * 256 + 256)
        hb = mm(gout[rows, :], ohi[...]) * st[rows, :]
        hi, lo = split(hb)
        g = mmt(latt[...], hi) + mmt(latt[...], lo)
        gin[:, :, :, rows] = g.reshape(8, 2, 16, 256)
        if n == 3:
            put(3, gin.at[:, 1 - core], gic, g_r.at[0], other)

    def gi1():
        arrived(gic, g_r.at[0])
        gin[:, core] = gin[:, core] + gic[...]
        for t in range(2):
            for k in (1, 3, 2):
                put(3, gin.at[t * 4 + lax.rem(y + k, 4), core], gid.at[t * 4 + y], g_r.at[1], ydev(k))
            gid[t * 4 + y] = gin[t * 4 + y, core]

    def gi1b():
        arrived(gid.at[pl.ds(0, 6)], g_r.at[1])
        for t in range(2):
            gic[t] = jnp.sum(gid[4 * t : 4 * t + 4], axis=0)
        put(3, gic.at[1 - zl], gio, g_r.at[5], zldev)

    def block(p):
        return pl.ds(pl.multiple_of(8 * lax.rem(p, 2), 8), 8), pl.ds(pl.multiple_of(128 * (p // 2), 128), 128)

    def gi2():
        arrived(gio, g_r.at[5])
        gic[2] = gic[zl] + gio[...]

        def go(k, carry):
            peer = lax.rem(ft + k, 16)
            r, l = block(peer)
            put(3, gic.at[2, r, l], gix.at[ft], g_r.at[2], (dp, peer))
            return carry

        lax.fori_loop(1, 16, go, 0)
        r, l = block(ft)
        gix[ft] = gic[2, r, l]

    def gi3():
        arrived(gix.at[pl.ds(0, 15)], g_r.at[2])
        r, l = block(ft)
        gig[r, l] = jnp.sum(gix[...], axis=0)

        def go(k, carry):
            put(3, gig.at[r, l], gig.at[r, l], g_r.at[3], (dp, lax.rem(ft + k, 16)))
            return carry

        lax.fori_loop(1, 16, go, 0)

    def gi4():
        arrived(gix.at[pl.ds(0, 15)], g_r.at[3])
        gi_ref[...] = gig[...]
        arrived(lvx.at[pl.ds(0, 15)], g_r.at[4])
        loss_ref[...] = jnp.sum(jnp.sum(lvx[...], axis=0), axis=(0, 1), keepdims=True) * (1.0 / 32768.0)

    steps = {"I": do_i, "A": do_a, "B": do_b, "D": do_d, "O1": go1, "O1b": go1b, "O2": go2, "O3": go3, "O4": go4,
             "K": back, "G1": gi1, "G1b": gi1b, "G2": gi2, "G3": gi3, "G4": gi4}
    for name, *where in ORDER:
        steps[name](*where)
    for s in range(NS):
        arrived(gfull.at[:, rows_of(s, 1 - core), :], o_r.at[s, 4])

    def turn(p, carry):
        v = gfull[pl.ds(p * 2, 2)].reshape(384, 128).T
        go_ref[:, pl.ds(pl.multiple_of(p * 384, 128), 384)] = jnp.where(core == 0, v[0:64], v[64:128])
        return carry

    lax.fori_loop(0, 8, turn, 0)
    for group, (rows, width) in enumerate(((576, 256), (15 * D_OWN, 256), (23 * D_OWN // 2, 256), (2280, 128))):
        arrived(part.at[pl.ds(0, rows), pl.ds(0, width)], send.at[group])


def hand_on(a, b, c, ao, bo, co):
    ao[...] = a[...]
    bo[...] = b[...]
    co[...] = c[...]


def per_device(images, labels, frequencies, privacy_noise, latents, gen_labels, gen_in, gen_out):
    vm = pl.BlockSpec(memory_space=pltpu.VMEM)
    hb = pl.BlockSpec(memory_space=pltpu.HBM)
    V = pltpu.VMEM
    dma = pltpu.SemaphoreType.DMA
    w = max(SUBS)
    h = w // 2
    scratch = [
        V((D, FL), BF16), V((HID, D), BF16), V((ROWS, D), BF16), V((10, 2, FL), F32), V((N, Z), BF16), V((Z, HID), BF16), V((32, FL), F32), V((N, HID), BF16),
        V((N, D), F32), V((D, N), F32), V((N, HID), F32), V((HID, N), F32), V((Z, N), BF16),
        V((32, ROWS), BF16), V((N, 128), BF16), V((N, FL), F32), V((N, FL), F32), V((32, FL), F32),
        V((16, 512), F32), V((16, 512), F32), V((8, 16, 512), F32), V((8, 16, 512), F32), V((32, 512), F32), V((32, 512), F32), V((N, FL), BF16), V((2, ROWS, 256), F32),
        V((D, N), F32), V((D, N), BF16), V((8, 2, 16, HID), F32),
        V((Q, 2, h, N), F32), V((Q, 2, w, N), F32), V((NS, 3, w, N), F32),
        V((8, 16, HID), F32), V((8, 16, HID), F32), V((16, HID), F32), V((16, 8, 128), F32), V((16, HID), F32), V((16, 8, 128), F32),
        V((NS, w, HID), F32), V((NS, h, HID), F32), V((NS, 8, h, 128), F32), V((NS, 2, h, 128), F32), V((NS, h, 128), F32), V((16, 192, 128), F32),
    ]
    sems = [dma((14,)), dma((4,)), dma((2, 3)), dma((Q,)), dma((Q,)), dma((NS,)), dma((6,)), dma((NS, 6))]
    loss, gi, go = pl.pallas_call(
        kernel,
        out_shape=(
            jax.ShapeDtypeStruct((1, 1), F32),
            jax.ShapeDtypeStruct((16, HID), F32),
            jax.ShapeDtypeStruct((64, D), F32),
        ),
        in_specs=[hb] * 6 + [vm] * 2,
        out_specs=(vm, vm, vm),
        scratch_shapes=scratch + sems,
        compiler_params=pltpu.CompilerParams(collective_id=0, has_side_effects=True, vmem_limit_bytes=58 << 20),
        cost_estimate=pl.CostEstimate(flops=12_000_000_000, bytes_accessed=17_000_000, transcendentals=2_000_000),
        name="feature_match",
    )(images, frequencies, gen_out, privacy_noise, latents, gen_in, labels, gen_labels)
    loss, gi, go = pl.pallas_call(
        hand_on,
        out_shape=(
            jax.ShapeDtypeStruct((1, 1), F32),
            jax.ShapeDtypeStruct((16, HID), F32),
            jax.ShapeDtypeStruct((64, D), F32),
        ),
        in_specs=[vm] * 3,
        out_specs=(vm,) * 3,
        name="hand_on",
    )(loss, gi, go)
    return loss.reshape(()), gi, go


def solution(mesh):
    return jax.shard_map(
        per_device,
        mesh=mesh,
        in_specs=(
            P("dp", None),
            P("dp"),
            P(None, "feat"),
            P(None, None, "feat"),
            P("dp", None),
            P("dp"),
            P(),
            P(),
        ),
        out_specs=(P(), P("dp", None), P("dp", None)),
        check_vma=False,
    )
```

```python
import functools

import jax
import jax.numpy as jnp
from jax import lax
from jax.experimental import pallas as pl
from jax.experimental.pallas import tpu as pltpu
from jax.sharding import PartitionSpec as P

MESH = pl.DeviceIdType.MESH
F32 = jnp.float32
BF16 = jnp.bfloat16

SIN = (6.28318284102346, -41.34142273936724, 81.59620932441723, -76.58030929887768, 41.20616782312917, -12.272323133322006)
COS = (0.999999989172567, -19.73920453212146, 64.93911898457917, -85.45016555726593, 60.16783176141255, -25.968313346422505, 6.5296104065360066)

N, D, FL, HID, Z, NI = 256, 3072, 1024, 1024, 256, 384
ROWS = N + NI
SUBS = (64, 32, 64, 32)
STARTS = (0, 64, 96, 160)
FIRST = ('x', 'z', 'x', 'x')
REL = (2, 1, 3, 0)
NS = len(SUBS)
D_OWN = sum(SUBS)
Q = 4 * NS
ORDER = (
    ("A", 0, 0),
    ("A", 0, 1),
    ("I", 2, 0),
    ("I", 2, 1),
    ("A", 0, 2),
    ("I", 2, 2),
    ("K", 0),
    ("A", 0, 3),
    ("A", 1, 0),
    ("K", 1),
    ("A", 1, 1),
    ("A", 1, 2),
    ("I", 2, 3),
    ("I", 3, 0),
    ("B", 0, 0),
    ("A", 1, 3),
    ("I", 3, 1),
    ("I", 3, 2),
    ("I", 3, 3),
    ("K", 2),
    ("B", 0, 1),
    ("A", 2, 0),
    ("K", 3),
    ("B", 1, 0),
    ("A", 2, 1),
    ("B", 0, 2),
    ("B", 1, 1),
    ("A", 2, 2),
    ("G1",),
    ("B", 0, 3),
    ("B", 1, 2),
    ("A", 2, 3),
    ("A", 3, 0),
    ("A", 3, 1),
    ("A", 3, 2),
    ("A", 3, 3),
    ("B", 2, 0),
    ("B", 1, 3),
    ("B", 2, 1),
    ("D", 0),
    ("B", 2, 2),
    ("D", 1),
    ("O1", 0),
    ("B", 2, 3),
    ("B", 3, 0),
    ("O1", 1),
    ("B", 3, 1),
    ("G1b",),
    ("B", 3, 2),
    ("B", 3, 3),
    ("D", 2),
    ("O1b", 0),
    ("O1", 2),
    ("O1b", 1),
    ("G2",),
    ("O2", 0),
    ("D", 3),
    ("O2", 1),
    ("O1", 3),
    ("O1b", 2),
    ("O3", 0),
    ("O2", 2),
    ("O3", 1),
    ("O2", 3),
    ("G3",),
    ("O4", 0),
    ("O3", 2),
    ("O4", 1),
    ("O4", 3),
    ("O4", 2),
    ("G4",),
)
NT = (((1,), (1,)), ((), ()))


def poly(coeffs, u):
    r = coeffs[-1] * u + coeffs[-2]
    for c in coeffs[-3::-1]:
        r = r * u + c
    return r


def cos_sin(phase):
    t = phase * 0.15915494309189535
    f = t - jnp.round(t)
    u = f * f
    return poly(COS, u), f * poly(SIN, u)


def split(v):
    hi = v.astype(BF16)
    return hi, (v - hi.astype(F32)).astype(BF16)


def mm(a, b):
    return jnp.dot(a, b, preferred_element_type=F32)


def mmt(a, b):
    return lax.dot_general(a, b, NT, preferred_element_type=F32)


def kernel(images_h, freq_h, gen_out_h, noise_h, lat_h, gin_h, lab_ref, glab_ref,
           loss_ref, gi_ref, go_ref,
           freq, gout, lhs, noise3, lat, gin_w, noise, hidden, q_s, qt, s_s, st, latt, oneh, onet, cosg, sing, gp, from_core0, from_core1, chips0, chips1, gap0, gap1, pg, ph,
           part, ohi, gin, xa, xb, zr, gic, gid, gio, gix, gig, lvx, gt_p, goc, god, goy, goz, gfull,
           lsem, send, ar_r, xa_r, xb_r, zr_r, g_r, o_r):
    dp = lax.axis_index("dp")
    ft = lax.axis_index("feat")
    core = lax.rem(dp, 2)
    chip = dp // 2
    x = ft // 4
    zh = lax.rem(ft, 4)

    def xdev(k):
        return (dp, lax.rem(x + k, 4) * 4 + zh)

    def zdev(k):
        return (dp, x * 4 + lax.rem(zh + k, 4))

    def cdev(k):
        return (lax.rem(chip + k, 8) * 2 + core, ft)

    other = (chip * 2 + 1 - core, ft)
    zl = chip // 4
    y = lax.rem(chip, 4)

    def ydev(k):
        return ((zl * 4 + lax.rem(y + k, 4)) * 2 + core, ft)

    zldev = (((1 - zl) * 4 + y) * 2 + core, ft)

    def put(group, src, dst, rs, dev):
        pltpu.make_async_remote_copy(
            src_ref=src, dst_ref=dst, send_sem=send.at[group], recv_sem=rs, device_id=dev, device_id_type=MESH
        ).start()

    def arrived(ref, rs):
        pltpu.make_async_copy(ref, ref, rs).wait()

    loads = [pltpu.make_async_copy(gen_out_h.at[:, pl.ds(n * 512, 512)], gout.at[:, pl.ds(n * 512, 512)], lsem.at[n]) for n in range(6)]
    loads.append(pltpu.make_async_copy(images_h, lhs.at[pl.ds(N, NI)], lsem.at[6]))
    for n in range(4):
        loads.append(pltpu.make_async_copy(freq_h.at[:, pl.ds(n * 256, 256)], freq.at[:, pl.ds(n * 256, 256)], lsem.at[7 + n]))
    loads.append(pltpu.make_async_copy(lat_h, lat, lsem.at[11]))
    loads.append(pltpu.make_async_copy(gin_h, gin_w, lsem.at[12]))
    loads.append(pltpu.make_async_copy(noise_h, noise3, lsem.at[13]))
    loads[11].start()
    loads[12].start()
    for n in range(6):
        loads[n].start()
    loads[13].start()

    bar = pltpu.get_barrier_semaphore()

    def greet(k, carry):
        pl.semaphore_signal(bar, inc=1, device_id=(lax.rem(dp + k, 16), ft), device_id_type=MESH)
        pl.semaphore_signal(bar, inc=1, device_id=(dp, lax.rem(ft + k, 16)), device_id_type=MESH)
        return carry

    lax.fori_loop(1, 16, greet, 0)

    cls = lax.broadcasted_iota(jnp.int32, (32, N), 0)
    on_g = (jnp.where(cls < 16, cls, cls - 16) == glab_ref[...][None, :]).astype(F32)
    cls_g = lax.broadcasted_iota(jnp.int32, (16, N), 0)
    oneh[0:16, 0:N] = (cls_g == glab_ref[...][None, :]).astype(F32).astype(BF16)
    oneh[16:32, 0:N] = jnp.zeros((16, N), BF16)
    cls_d = lax.broadcasted_iota(jnp.int32, (16, NI), 0)
    oneh[0:16, N:ROWS] = jnp.zeros((16, NI), BF16)
    oneh[16:32, N:ROWS] = (cls_d == lab_ref[...][None, :]).astype(F32).astype(BF16)
    onet[...] = jnp.concatenate([on_g, jnp.zeros((96, N), F32)], axis=0).T.astype(BF16)
    loads[11].wait()
    latt[...] = lat[...].astype(F32).T.astype(BF16)
    loads[12].wait()

    pre = mm(lat[...], gin_w[...])
    sig = jax.nn.sigmoid(pre)
    hidden[...] = (pre * sig).astype(BF16)
    s_s[...] = sig * (1.0 + pre * (1.0 - sig))

    for n in range(6):
        loads[n].wait()
        if n < 5:
            loads[6 + n].start()
        cols = slice(n * 512, n * 512 + 512)
        out = jnp.tanh(mm(hidden[...], gout[:, cols]))
        lhs[0:N, cols] = out.astype(BF16)
        q_s[:, cols] = 1.0 - out * out
    loads[6].wait()

    def phase(n):
        loads[7 + n].wait()
        ph[n % 2] = mm(lhs[...], freq[:, n * 256 : n * 256 + 256])

    def sums(n):
        cols = slice(n * 256, n * 256 + 256)
        cs, sn = cos_sin(ph[n % 2])
        cosg[:, cols] = cs[0:N]
        sing[:, cols] = sn[0:N]
        for k, v in ((0, cs), (1, sn)):
            hi, lo = split(v)
            total = mm(oneh[...], hi) + mm(oneh[...], lo)
            gp[16 * k : 16 * k + 16, cols] = total[0:16] * (10.0 / 4096.0) - total[16:32] * (10.0 / 6144.0)

    parts = ((slice(0, 512), from_core0, chips0, gap0), (slice(512, 1024), from_core1, chips1, gap1))
    own_rows = pl.ds(pl.multiple_of(16 * core, 16), 16)
    other_rows = pl.ds(pl.multiple_of(16 * (1 - core), 16), 16)

    def ar1(h):
        cols, got, _, _ = parts[h]
        put(0, gp.at[other_rows, cols], got, ar_r.at[h, 0], other)

    def ar2(h):
        cols, got, chips, _ = parts[h]
        arrived(got, ar_r.at[h, 0])
        chips[chip] = gp[own_rows, cols] + got[...]
        for k in range(1, 8):
            put(0, chips.at[chip], chips.at[chip], ar_r.at[h, 1], cdev(k))

    def ar3(h):
        _, _, chips, whole = parts[h]
        arrived(chips.at[pl.ds(0, 7)], ar_r.at[h, 1])
        whole[own_rows, :] = jnp.sum(chips[...], axis=0)
        put(0, whole.at[own_rows], whole.at[own_rows], ar_r.at[h, 2], other)

    def gap(h):
        cols, _, _, whole = parts[h]
        arrived(whole.at[other_rows], ar_r.at[h, 2])
        g = whole[...] - noise[:, cols]
        sq = g * g
        lv = sq[0:8] + sq[8:16] + sq[16:24] + sq[24:32]
        lv = sum(lv[:, i : i + 128] for i in range(0, lv.shape[1], 128))
        hi, lo = split(g * (160.0 / 4096.0))
        g0 = mm(onet[:, 0:32], jnp.concatenate([hi[0:16], lo[0:16]], axis=0))
        g1 = mm(onet[:, 0:32], jnp.concatenate([hi[16:32], lo[16:32]], axis=0))
        pg[:, cols] = (cosg[:, cols] * g1 - sing[:, cols] * g0).astype(BF16)
        return lv

    phase(0)
    phase(1)
    sums(0)
    phase(2)
    sums(1)
    pl.semaphore_wait(bar, 30)
    ar1(0)
    phase(3)
    sums(2)
    ar2(0)
    sums(3)
    ar1(1)
    ar2(1)

    def turn_q(n, carry):
        o = pl.multiple_of(n * 256, 256)
        qt[pl.ds(o, 256), :] = q_s[:, pl.ds(o, 256)].T
        return carry

    lax.fori_loop(0, 12, turn_q, 0)
    ar3(0)
    loads[13].wait()
    noise[...] = jnp.zeros_like(noise)
    for k in range(2):
        noise[16 * k : 16 * k + 10, :] = noise3[:, k, :]

    def turn_s(n, carry):
        o = pl.multiple_of(n * 256, 256)
        st[pl.ds(o, 256), :] = s_s[:, pl.ds(o, 256)].T
        return carry

    lax.fori_loop(0, 4, turn_s, 0)
    lv = gap(0)

    ar3(1)

    def first_half(n, carry):
        rows = pl.ds(pl.multiple_of(n * 768, 256), 768)
        part[rows, :] = mmt(freq[rows, 0:512], pg[:, 0:512])
        return carry

    lax.fori_loop(0, 4, first_half, 0)

    lv = lv + gap(1)

    def rows_at(r1, r2, s, half, rows):
        xr, zr = (r1, r2) if FIRST[s] == "x" else (r2, r1)
        base = lax.rem(x + xr, 4) * 768 + lax.rem(zh + zr, 4) * 192 + STARTS[s] + half
        return part.at[pl.ds(pl.multiple_of(base, 8), rows), :]

    def dev1(s, k):
        return xdev(k) if FIRST[s] == "x" else zdev(k)

    def dev2(s, k):
        return zdev(k) if FIRST[s] == "x" else xdev(k)

    def second_half(xr):
        rows = pl.ds(pl.multiple_of(lax.rem(x + xr, 4) * 768, 256), 768)
        part[rows, :] += mmt(freq[rows, 512:1024], pg[:, 512:1024])

    def do_i(s, k):
        h, q = SUBS[s] // 2, s * 4 + k
        for b in range(2):
            put(1, rows_at(2, REL[k], s, b * h, h), xa.at[q, b, pl.ds(0, h)], xa_r.at[q], dev1(s, (1, 3)[b]))

    def do_a(s, k):
        w, q = SUBS[s], s * 4 + k
        h = w // 2
        arrived(xa.at[q, :, pl.ds(0, h)], xa_r.at[q])
        for b in range(2):
            r = rows_at((1, 3)[b], REL[k], s, b * h, h)
            r[...] = r[...] + xa[q, b, 0:h]
            put(1, rows_at((1, 3)[b], REL[k], s, 0, w), xb.at[q, b, pl.ds(0, w)], xb_r.at[q], dev1(s, (1, 3)[b]))

    def do_b(s, k):
        w, q = SUBS[s], s * 4 + k
        arrived(xb.at[q, :, pl.ds(0, w)], xb_r.at[q])
        r = rows_at(0, REL[k], s, 0, w)
        r[...] = r[...] + xb[q, 0, 0:w] + xb[q, 1, 0:w]
        if k < 3:
            put(1, r, zr.at[s, k, pl.ds(0, w)], zr_r.at[s], dev2(s, REL[k]))

    def do_d(s):
        w = SUBS[s]
        arrived(zr.at[s, :, pl.ds(0, w)], zr_r.at[s])
        own = rows_at(0, 0, s, 0, w)[...] + zr[s, 0, 0:w] + zr[s, 1, 0:w] + zr[s, 2, 0:w]
        base = pl.multiple_of(ft * 192 + STARTS[s], 8)
        og = (own * qt[pl.ds(base, w), :]).astype(BF16)
        gt_p[s, 0:w, :] = mm(og, hidden[...])
        h = w // 2
        put(2, gt_p.at[s, pl.ds(pl.multiple_of((1 - core) * h, 8), h)], goc.at[s, pl.ds(0, h)], o_r.at[s, 0], other)

    second_half(2)
    for s in range(NS):
        if FIRST[s] == "x" and s < 1:
            for k in range(4):
                do_i(s, k)

    lvx[ft] = lv
    def tell(k, carry):
        put(3, lvx.at[ft], lvx.at[ft], g_r.at[4], (dp, lax.rem(ft + k, 16)))
        return carry

    lax.fori_loop(1, 16, tell, 0)
    for xr in (1, 3, 0):
        second_half(xr)
    for s in range(NS):
        if FIRST[s] == "z":
            for k in range(4):
                do_i(s, k)

    def factor(n, carry):
        rows = pl.ds(pl.multiple_of(n * 256, 256), 256)
        ohi[rows, :] = (part[rows, :] * qt[rows, :]).astype(BF16)
        return carry

    lax.fori_loop(0, 12, factor, 0)

    def rows_of(s, c):
        h = SUBS[s] // 2
        return pl.ds(pl.multiple_of(STARTS[s] + c * h, 8), h)

    def go1(s):
        h = SUBS[s] // 2
        mine = pl.ds(pl.multiple_of(core * h, 8), h)
        arrived(goc.at[s, pl.ds(0, h)], o_r.at[s, 0])
        r = gt_p.at[s, mine]
        r[...] = r[...] + goc[s, 0:h]
        if s == NS - 1:
            for k in range(1, 8):
                peer = lax.rem(chip + k, 8)
                put(2, gt_p.at[s, mine, pl.ds(pl.multiple_of(peer * 128, 128), 128)], god.at[s, chip, pl.ds(0, h)], o_r.at[s, 1], cdev(k))
            god[s, chip, 0:h] = gt_p[s, mine, pl.ds(pl.multiple_of(chip * 128, 128), 128)]
            return
        for t in range(2):
            for k in (1, 3, 2):
                cols = pl.ds(pl.multiple_of((t * 4 + lax.rem(y + k, 4)) * 128, 128), 128)
                put(2, gt_p.at[s, mine, cols], god.at[s, t * 4 + y, pl.ds(0, h)], o_r.at[s, 1], ydev(k))
            god[s, t * 4 + y, 0:h] = gt_p[s, mine, pl.ds(pl.multiple_of((t * 4 + y) * 128, 128), 128)]

    def go1b(s):
        h = SUBS[s] // 2
        arrived(god.at[s, pl.ds(0, 6), pl.ds(0, h)], o_r.at[s, 1])
        for t in range(2):
            goy[s, t, 0:h] = jnp.sum(god[s, 4 * t : 4 * t + 4, 0:h], axis=0)
        put(2, goy.at[s, 1 - zl, pl.ds(0, h)], goz.at[s, pl.ds(0, h)], o_r.at[s, 5], zldev)

    def go2(s):
        h = SUBS[s] // 2
        if s == NS - 1:
            arrived(god.at[s, pl.ds(0, 7), pl.ds(0, h)], o_r.at[s, 1])
            gfull[ft, rows_of(s, core), :] = jnp.sum(god[s, :, 0:h], axis=0)
        else:
            arrived(goz.at[s, pl.ds(0, h)], o_r.at[s, 5])
            gfull[ft, rows_of(s, core), :] = goy[s, zl, 0:h] + goz[s, 0:h]
        at = gfull.at[ft, rows_of(s, core), :]
        if s < NS - 1:
            for k in (1, 3, 2):
                put(2, at, at, o_r.at[s, 2], zdev(k))
        else:

            def go(k, carry):
                put(2, at, at, o_r.at[s, 3], (dp, lax.rem(ft + k, 16)))
                return carry

            lax.fori_loop(1, 16, go, 0)

    def go3(s):
        h = SUBS[s] // 2
        arrived(god.at[s, pl.ds(0, 3), pl.ds(0, h)], o_r.at[s, 2])
        at = gfull.at[pl.ds(x * 4, 4), rows_of(s, core), :]
        for k in (1, 3, 2):
            put(2, at, at, o_r.at[s, 3], xdev(k))

    def go4(s):
        arrived(gfull.at[pl.ds(0, 12 if s < NS - 1 else 15), rows_of(s, core), :], o_r.at[s, 3])
        at = gfull.at[:, rows_of(s, core), :]
        put(2, at, at, o_r.at[s, 4], other)

    def back(n):
        rows = slice(n * 256, n * 256 + 256)
        hb = mm(gout[rows, :], ohi[...]) * st[rows, :]
        hi, lo = split(hb)
        g = mmt(latt[...], hi) + mmt(latt[...], lo)
        gin[:, :, :, rows] = g.reshape(8, 2, 16, 256)
        if n == 3:
            put(3, gin.at[:, 1 - core], gic, g_r.at[0], other)

    def gi1():
        arrived(gic, g_r.at[0])
        gin[:, core] = gin[:, core] + gic[...]
        for t in range(2):
            for k in (1, 3, 2):
                put(3, gin.at[t * 4 + lax.rem(y + k, 4), core], gid.at[t * 4 + y], g_r.at[1], ydev(k))
            gid[t * 4 + y] = gin[t * 4 + y, core]

    def gi1b():
        arrived(gid.at[pl.ds(0, 6)], g_r.at[1])
        for t in range(2):
            gic[t] = jnp.sum(gid[4 * t : 4 * t + 4], axis=0)
        put(3, gic.at[1 - zl], gio, g_r.at[5], zldev)

    def block(p):
        return pl.ds(pl.multiple_of(8 * lax.rem(p, 2), 8), 8), pl.ds(pl.multiple_of(128 * (p // 2), 128), 128)

    def gi2():
        arrived(gio, g_r.at[5])
        gic[2] = gic[zl] + gio[...]

        def go(k, carry):
            peer = lax.rem(ft + k, 16)
            r, l = block(peer)
            put(3, gic.at[2, r, l], gix.at[ft], g_r.at[2], (dp, peer))
            return carry

        lax.fori_loop(1, 16, go, 0)
        r, l = block(ft)
        gix[ft] = gic[2, r, l]

    def gi3():
        arrived(gix.at[pl.ds(0, 15)], g_r.at[2])
        r, l = block(ft)
        gig[r, l] = jnp.sum(gix[...], axis=0)

        def go(k, carry):
            put(3, gig.at[r, l], gig.at[r, l], g_r.at[3], (dp, lax.rem(ft + k, 16)))
            return carry

        lax.fori_loop(1, 16, go, 0)

    def gi4():
        arrived(gix.at[pl.ds(0, 15)], g_r.at[3])
        gi_ref[...] = gig[...]
        arrived(lvx.at[pl.ds(0, 15)], g_r.at[4])
        loss_ref[...] = jnp.sum(jnp.sum(lvx[...], axis=0), axis=(0, 1), keepdims=True) * (1.0 / 32768.0)

    steps = {"I": do_i, "A": do_a, "B": do_b, "D": do_d, "O1": go1, "O1b": go1b, "O2": go2, "O3": go3, "O4": go4,
             "K": back, "G1": gi1, "G1b": gi1b, "G2": gi2, "G3": gi3, "G4": gi4}
    for name, *where in ORDER:
        steps[name](*where)
    for s in range(NS):
        arrived(gfull.at[:, rows_of(s, 1 - core), :], o_r.at[s, 4])

    def turn(p, carry):
        v = gfull[pl.ds(p * 2, 2)].reshape(384, 128).T
        go_ref[:, pl.ds(pl.multiple_of(p * 384, 128), 384)] = jnp.where(core == 0, v[0:64], v[64:128])
        return carry

    lax.fori_loop(0, 8, turn, 0)
    for group, (rows, width) in enumerate(((576, 256), (15 * D_OWN, 256), (23 * D_OWN // 2, 256), (2280, 128))):
        arrived(part.at[pl.ds(0, rows), pl.ds(0, width)], send.at[group])


def hand_on(a, b, c, ao, bo, co):
    ao[...] = a[...]
    bo[...] = b[...]
    co[...] = c[...]


def per_device(images, labels, frequencies, privacy_noise, latents, gen_labels, gen_in, gen_out):
    vm = pl.BlockSpec(memory_space=pltpu.VMEM)
    hb = pl.BlockSpec(memory_space=pltpu.HBM)
    V = pltpu.VMEM
    dma = pltpu.SemaphoreType.DMA
    w = max(SUBS)
    h = w // 2
    scratch = [
        V((D, FL), BF16), V((HID, D), BF16), V((ROWS, D), BF16), V((10, 2, FL), F32), V((N, Z), BF16), V((Z, HID), BF16), V((32, FL), F32), V((N, HID), BF16),
        V((N, D), F32), V((D, N), F32), V((N, HID), F32), V((HID, N), F32), V((Z, N), BF16),
        V((32, ROWS), BF16), V((N, 128), BF16), V((N, FL), F32), V((N, FL), F32), V((32, FL), F32),
        V((16, 512), F32), V((16, 512), F32), V((8, 16, 512), F32), V((8, 16, 512), F32), V((32, 512), F32), V((32, 512), F32), V((N, FL), BF16), V((2, ROWS, 256), F32),
        V((D, N), F32), V((D, N), BF16), V((8, 2, 16, HID), F32),
        V((Q, 2, h, N), F32), V((Q, 2, w, N), F32), V((NS, 3, w, N), F32),
        V((8, 16, HID), F32), V((8, 16, HID), F32), V((16, HID), F32), V((16, 8, 128), F32), V((16, HID), F32), V((16, 8, 128), F32),
        V((NS, w, HID), F32), V((NS, h, HID), F32), V((NS, 8, h, 128), F32), V((NS, 2, h, 128), F32), V((NS, h, 128), F32), V((16, 192, 128), F32),
    ]
    sems = [dma((14,)), dma((4,)), dma((2, 3)), dma((Q,)), dma((Q,)), dma((NS,)), dma((6,)), dma((NS, 6))]
    loss, gi, go = pl.pallas_call(
        kernel,
        out_shape=(
            jax.ShapeDtypeStruct((1, 1), F32),
            jax.ShapeDtypeStruct((16, HID), F32),
            jax.ShapeDtypeStruct((64, D), F32),
        ),
        in_specs=[hb] * 6 + [vm] * 2,
        out_specs=(vm, vm, vm),
        scratch_shapes=scratch + sems,
        compiler_params=pltpu.CompilerParams(collective_id=0, has_side_effects=True, vmem_limit_bytes=58 << 20),
        cost_estimate=pl.CostEstimate(flops=12_000_000_000, bytes_accessed=17_000_000, transcendentals=2_000_000),
        name="feature_match",
    )(images, frequencies, gen_out, privacy_noise, latents, gen_in, labels, gen_labels)
    loss, gi, go = pl.pallas_call(
        hand_on,
        out_shape=(
            jax.ShapeDtypeStruct((1, 1), F32),
            jax.ShapeDtypeStruct((16, HID), F32),
            jax.ShapeDtypeStruct((64, D), F32),
        ),
        in_specs=[vm] * 3,
        out_specs=(vm,) * 3,
        name="hand_on",
    )(loss, gi, go)
    return loss.reshape(()), gi, go


def solution(mesh):
    return jax.shard_map(
        per_device,
        mesh=mesh,
        in_specs=(
            P("dp", None),
            P("dp"),
            P(None, "feat"),
            P(None, None, "feat"),
            P("dp", None),
            P("dp"),
            P(),
            P(),
        ),
        out_specs=(P(), P("dp", None), P("dp", None)),
        check_vma=False,
    )
```
